256 devices in a mesh: step: 16 (over y, x), cfg: 2 (over core), seq: 8 (over z).
Axes of the slice: x: 4, y: 4, z: 8, core: 2. Of those that a mesh axis runs over, the one named last changes fastest.
Arguments:
- initial_noisy_clip: float32 [2048, 1024], P('seq'), may hold values from -6 to 6
- sampler_noise_level_ordinal: int32 [16], P('step'), may hold values from 0 to 49
- classifier_free_strength: float32 [16], P('step'), may hold values from 1.5 to 4
- integrator_increment: float32 [16], P('step'), may hold values from 0.03 to 0.12
- noise_level_affine_gates: bfloat16 [50, 3072], replicated, may hold values from -3 to 3
- guided_affine_gate_pairs: bfloat16 [2, 3072], P('cfg'), may hold values from -3 to 3
- attention_input_projectors: bfloat16 [1024, 3072], replicated, may hold values from -0.1875 to 0.1875
- attention_merge_projector: bfloat16 [1024, 1024], replicated, may hold values from -0.1875 to 0.1875
- attention_sharpness: float32 [16], replicated, may hold values from 1 to 4
Outputs:
- trajectory: float32 [16, 2048, 1024], P('step', 'seq')
The draws below stay inside these ranges and needn't reach their ends.
All inputs are finite; a program needn't handle non-finite values.
Results may differ from the reference program's by a relative error of at most 0.0045.
Values may be sent and summed in bfloat16 or wider, within the bound.
A program may use at most 128 MiB of HBM per device.

```python
import math
import jax
import jax.numpy as jnp
from jax import lax

D = 1024
ATTENTION_GROUPS = 16
NT = 50
SWEEPS = 2
STEPS = 16
FRAMES = 2048


def with_ends(array, own_key, low, high):
    longest = array.shape.index(max(array.shape))
    spots = []
    for shift in (0, 1):
        where = [jax.random.randint(jax.random.fold_in(own_key, axis), (), 0, length) for axis, length in enumerate(array.shape)]
        where[longest] = (where[longest] + shift) % array.shape[longest]
        spots.append(tuple(where))
    return array.at[spots[0]].set(low).at[spots[1]].set(high)


def shard_levels(key, dims, cuts, low, top_value):
    def one(position, blocks):
        steps = jax.random.uniform(jax.random.fold_in(jax.random.fold_in(key, 6), position), (blocks,), jnp.float32, low / len(cuts), top_value / len(cuts))
        return jnp.repeat(jnp.exp(steps), dims[position] // blocks).reshape((-1,) + (1,) * (len(dims) - position - 1))

    factor_of = one(*cuts[0])
    for cut in cuts[1:]:
        factor_of = factor_of * one(*cut)
    return factor_of


def scatter_about(stream_key, dims, scale, reach, shards=(), dtype=jnp.bfloat16):
    level = shard_levels(stream_key, dims, shards, -0.22, 0.18) if shards else 1.0
    drawn = jax.random.normal(stream_key, dims, jnp.float32) * scale * level
    return jnp.minimum(jnp.maximum(drawn, -reach), reach).astype(dtype)


def setup_inputs(seed: int = 0) -> dict:
    key_of = jax.random.split(jax.random.key(seed), 10)
    initial_noisy_clip = scatter_about(key_of[0], (FRAMES, D), 1.0, 6.0, ((0, 8),), jnp.float32)
    sampler_noise_level_ordinal = with_ends(jax.random.randint(key_of[1], (STEPS,), 0, NT), jax.random.fold_in(key_of[1], 1), 0, NT - 1).astype(jnp.int32)
    classifier_free_strength = jnp.clip(1.5 + 2.5 * jax.random.uniform(key_of[2], (STEPS,), jnp.float32) ** shard_levels(key_of[2], (STEPS,), ((0, 16),), -0.2, 0.2), 1.5, 4.0)
    integrator_increment = jnp.clip(jnp.exp(math.log(0.12) - 1.3862944 * jax.random.uniform(key_of[3], (STEPS,), jnp.float32) ** shard_levels(key_of[3], (STEPS,), ((0, 16),), -0.2, 0.2)), 0.03, 0.12)
    noise_level_affine_gates = scatter_about(key_of[4], (NT, 3 * D), 0.5, 3.0)
    guided_affine_gate_pairs = scatter_about(key_of[5], (2, 3 * D), 0.5, 3.0, ((0, 2),))
    attention_input_projectors = scatter_about(key_of[6], (D, 3 * D), D ** -0.5, 0.1875)
    attention_merge_projector = scatter_about(key_of[7], (D, D), D ** -0.5, 0.1875)
    attention_sharpness = jnp.clip(jnp.exp(jax.random.uniform(key_of[8], (ATTENTION_GROUPS,), jnp.float32, math.log(1.0), math.log(4.0))), 1.0, 4.0)
    return dict(initial_noisy_clip=initial_noisy_clip, sampler_noise_level_ordinal=sampler_noise_level_ordinal, classifier_free_strength=classifier_free_strength, integrator_increment=integrator_increment, noise_level_affine_gates=noise_level_affine_gates, guided_affine_gate_pairs=guided_affine_gate_pairs, attention_input_projectors=attention_input_projectors, attention_merge_projector=attention_merge_projector, attention_sharpness=attention_sharpness)


def paired_denoiser_estimates(noisy_pose_sequence, affine_gate_entries, attention_input_projectors, attention_merge_projector, attention_sharpness):
    frames = noisy_pose_sequence.shape[0]
    width = noisy_pose_sequence.shape[1]
    subspace_dimension = width // ATTENTION_GROUPS
    shift = affine_gate_entries[:width]
    scale_part = affine_gate_entries[width:2 * width]
    gate = affine_gate_entries[2 * width:]
    average = lax.optimization_barrier(jnp.mean(noisy_pose_sequence, axis=-1, keepdims=True))
    centred = noisy_pose_sequence - average
    variance = lax.optimization_barrier(jnp.mean(centred * centred, axis=-1, keepdims=True))
    normed = centred * lax.rsqrt(variance + 1e-06)
    hidden = (normed * (1.0 + scale_part) + shift).astype(jnp.bfloat16)
    qkv = jnp.dot(hidden, attention_input_projectors, preferred_element_type=jnp.float32).reshape(frames, 3, ATTENTION_GROUPS, subspace_dimension)
    raw_probe_vectors = qkv[:, 0]
    raw_k = qkv[:, 1]
    probe_vectors_stacked = raw_probe_vectors * lax.rsqrt(lax.optimization_barrier(jnp.mean(raw_probe_vectors * raw_probe_vectors, axis=-1, keepdims=True)) + 1e-06) * (attention_sharpness[:, None] / math.sqrt(subspace_dimension))
    probe_vectors_stacked = probe_vectors_stacked.astype(jnp.bfloat16)
    key_rows = (raw_k * lax.rsqrt(lax.optimization_barrier(jnp.mean(raw_k * raw_k, axis=-1, keepdims=True)) + 1e-06)).astype(jnp.bfloat16)
    value_rows = qkv[:, 2].astype(jnp.bfloat16)
    scores = jnp.einsum('qhd,khd->hqk', probe_vectors_stacked.astype(jnp.float32), key_rows.astype(jnp.float32))
    row_max = lax.optimization_barrier(jnp.max(scores, axis=-1, keepdims=True))
    powers = jnp.exp(scores - row_max)
    weights = (powers / lax.optimization_barrier(jnp.sum(powers, axis=-1, keepdims=True))).astype(jnp.bfloat16)
    attended = jnp.einsum('hqk,khd->qhd', weights.astype(jnp.float32), value_rows.astype(jnp.float32))
    attended = attended.astype(jnp.bfloat16).reshape(frames, width)
    projected = jnp.dot(attended, attention_merge_projector, preferred_element_type=jnp.float32)
    return (gate * projected).astype(jnp.bfloat16)

def reference(initial_noisy_clip, sampler_noise_level_ordinal, classifier_free_strength, integrator_increment, noise_level_affine_gates, guided_affine_gate_pairs, attention_input_projectors, attention_merge_projector, attention_sharpness):

    def slot_drift(inputs):
        noisy_pose_sequence, index_now, scale_now, step_now = inputs
        timestep_row = noise_level_affine_gates[index_now].astype(jnp.float32)
        transformer_block_returns = []
        for branch_index in range(2):
            affine_gate_entries = timestep_row + guided_affine_gate_pairs[branch_index].astype(jnp.float32)
            transformer_block_returns.append(paired_denoiser_estimates(noisy_pose_sequence, affine_gate_entries, attention_input_projectors, attention_merge_projector, attention_sharpness).astype(jnp.float32))
        guided = noisy_pose_sequence + scale_now * transformer_block_returns[0] + (1.0 - scale_now) * transformer_block_returns[1]
        return step_now * guided
    states = jnp.broadcast_to(initial_noisy_clip[None], (STEPS,) + initial_noisy_clip.shape)
    inclusive = states
    for sweep_index in range(SWEEPS):
        drifts = lax.map(slot_drift, (states, sampler_noise_level_ordinal, classifier_free_strength, integrator_increment))
        inclusive = jnp.cumsum(drifts, axis=0)
        exclusive = jnp.concatenate([jnp.zeros_like(inclusive[:1]), inclusive[:-1]], axis=0)
        states = initial_noisy_clip[None] + exclusive
    return initial_noisy_clip[None] + inclusive
```

```python
import math

import jax
import jax.numpy as jnp
from jax import lax
from jax.experimental import pallas as pl
from jax.experimental.pallas import tpu as pltpu
from jax.sharding import PartitionSpec as P

MESH = pl.DeviceIdType.MESH
F32 = jnp.float32
BF16 = jnp.bfloat16
LOG2E = 1.4426950408889634

WIDTH = 1024
FRAMES = 2048
CHUNK = 128
TILE = 256
RING = 8
STEPS = 16
COLUMN = 16


def remote(src, dst, send_sem, recv_sem, device):
    return pltpu.make_async_remote_copy(
        src_ref=src,
        dst_ref=dst,
        send_sem=send_sem,
        recv_sem=recv_sem,
        device_id=device,
        device_id_type=MESH,
    )


def fold(rows):
    half = WIDTH // 2
    return jnp.concatenate([rows[:, :, :half], rows[:, :, half:]], axis=1).astype(BF16)


def unfold(tiles):
    wide = tiles.astype(F32)
    return jnp.concatenate([wide[:, :8], wide[:, 8:]], axis=2)


def layer_norm(rows):
    average = jnp.mean(rows, axis=-1, keepdims=True)
    centred = rows - average
    variance = jnp.mean(centred * centred, axis=-1, keepdims=True)
    return centred * lax.rsqrt(variance + 1e-06)


def kernel(
    clip_ref,
    ordinal_ref,
    strength_ref,
    increment_ref,
    table_ref,
    pair_ref,
    w_in_ref,
    w_merge_ref,
    sharp_ref,
    out_ref,
    xall,
    w_raw,
    w_mod,
    w_out,
    bias,
    qb,
    kb,
    vb,
    acc,
    ob,
    att,
    sb,
    rb,
    nb,
    nr,
    fin,
    states,
    gates,
    incs,
    local_sem,
    maj_send,
    min_send,
    d2d_send,
    ring_recv,
    a2a_send,
    a2a_recv,
    s_send,
    s_recv,
    n_send,
    n_recv,
    inc_send,
    inc_recv,
    pair_send,
    pair_recv,
):
    k = lax.axis_index("step")
    c = lax.axis_index("cfg")
    z = lax.axis_index("seq")
    other = 1 - c
    sign = 1 - 2 * c
    mine = 2 * z + c

    barrier = pltpu.get_barrier_semaphore()

    def greet(o, carry):
        e = lax.rem(mine + o, COLUMN)
        pl.semaphore_signal(
            barrier, inc=1, device_id={"seq": e // 2, "cfg": lax.rem(e, 2)}, device_id_type=MESH
        )
        pl.semaphore_signal(
            barrier, inc=1, device_id={"step": lax.rem(k + o, STEPS)}, device_id_type=MESH
        )
        return carry

    lax.fori_loop(1, COLUMN, greet, 0)

    loads = []
    for part in range(3):
        columns = pl.ds(pl.multiple_of(part * WIDTH + z * 128, 128), 128)
        loads.append(
            pltpu.make_async_copy(
                w_in_ref.at[:, columns], w_raw.at[part], local_sem.at[part]
            )
        )
    loads.append(pltpu.make_async_copy(w_merge_ref, w_out, local_sem.at[3]))
    for load in loads:
        load.start()

    own_rows = pl.ds(pl.multiple_of(c * CHUNK, CHUNK), CHUNK)
    xall[0, mine] = layer_norm(clip_ref[own_rows, :]).astype(BF16)

    lane = lax.broadcasted_iota(jnp.int32, (1, 128), 1)
    first_head = lane < 64

    pl.semaphore_wait(barrier, 2 * (COLUMN - 1))

    def slot(zz, cc):
        return 2 * zz + cc

    def ring(t, index, send_sem, zz):
        block = xall.at[t, index]
        return remote(block, block, send_sem, ring_recv.at[t, index], {"seq": zz})

    def across(t, index, i):
        block = xall.at[t, index]
        return remote(block, block, d2d_send.at[t, i], ring_recv.at[t, index], {"cfg": other})

    z_major = lax.rem(z + sign + RING, RING)
    z_minor = lax.rem(z - sign + RING, RING)

    def begin(t):
        ring(t, mine, maj_send.at[t, 0], z_major).start()
        ring(t, mine, min_send.at[t, 0], z_minor).start()
        across(t, mine, 0).start()

    begin(0)

    chosen = (
        lax.broadcasted_iota(jnp.int32, (16, table_ref.shape[0]), 1) == ordinal_ref[0]
    ).astype(BF16)
    affine = jnp.dot(chosen, table_ref[...], preferred_element_type=F32)[:8] + pair_ref[
        ...
    ].astype(F32)
    shift = affine[:, :WIDTH]
    scale_now = strength_ref[0]
    step_now = increment_ref[0]
    share = jnp.where(c == 0, scale_now, 1.0 - scale_now) * step_now
    gates[c] = affine[:, 2 * WIDTH :] * share
    incs[k] = jnp.full((8, 128), step_now, F32)
    gate_copy = remote(
        gates.at[c], gates.at[c], pair_send.at[0], pair_recv.at[0], {"cfg": other}
    )
    gate_copy.start()

    def inc_copy(o):
        return remote(
            incs.at[k],
            incs.at[k],
            inc_send.at[o],
            inc_recv.at[k],
            {"step": lax.rem(k + o, STEPS)},
        )

    def send_inc(o, carry):
        inc_copy(o).start()
        return carry

    lax.fori_loop(1, STEPS, send_inc, 0)

    scale_column = jnp.transpose(
        jnp.broadcast_to(1.0 + affine[:1, WIDTH : 2 * WIDTH], (128, WIDTH))
    )
    shift_high = shift.astype(BF16)
    shift_low = shift - shift_high.astype(F32)
    shift_parts = jnp.concatenate([shift_high.astype(F32), shift_low], axis=0).astype(BF16)
    for part in range(3):
        loads[part].wait()
        raw = w_raw[part]
        both = jnp.dot(shift_parts, raw, preferred_element_type=F32)
        bias[:, part * 128 : (part + 1) * 128] = both[:8] + both[8:]
        w_mod[:, part * 128 : (part + 1) * 128] = (raw.astype(F32) * scale_column).astype(BF16)
    ones = jnp.ones((1, 128), F32)
    for h in range(2):
        mask = first_head if h == 0 else jnp.logical_not(first_head)
        vb[h, :, 128:] = jnp.broadcast_to(jnp.where(mask, ones, 0.0), (FRAMES, 128)).astype(BF16)
    q_scale = jnp.where(first_head, sharp_ref[2 * z], sharp_ref[2 * z + 1]) * (
        LOG2E / math.sqrt(64.0)
    )
    same_head = (
        (lax.broadcasted_iota(jnp.int32, (128, 128), 0) < 64)
        == (lax.broadcasted_iota(jnp.int32, (128, 128), 1) < 64)
    ).astype(F32).astype(BF16)

    def project(t, start, slots):
        rows = len(slots) * CHUNK
        block = jnp.concatenate([xall[t, s] for s in slots], axis=0)
        qkv = jnp.dot(block, w_mod[...], preferred_element_type=F32) + bias[:1, :]
        here = pl.ds(start, rows)

        def normalize(values):
            squares = jnp.dot(
                (values * values).astype(BF16), same_head, preferred_element_type=F32
            )
            return values * lax.rsqrt(squares * (1.0 / 64.0) + 1e-06)

        qb[here, :] = (normalize(qkv[:, :128]) * q_scale).astype(BF16)
        keys = normalize(qkv[:, 128:256])
        values = qkv[:, 256:]
        for h in range(2):
            mask = first_head if h == 0 else jnp.logical_not(first_head)
            kb[h, here, :] = jnp.where(mask, keys, 0.0).astype(BF16)
            vb[h, here, :128] = jnp.where(mask, values, 0.0).astype(BF16)

    def attend(q_start, low, high, total):
        q = qb[pl.ds(q_start, TILE), :]
        for j in range(low, high, 256):
            for h in range(2):
                scores = lax.dot_general(
                    q, kb[h, j : j + 256, :], (((1,), (1,)), ((), ())), preferred_element_type=F32
                )
                powers = jnp.exp2(scores).astype(BF16)
                total = total + jnp.dot(
                    powers, vb[h, j : j + 256, :], preferred_element_type=F32
                )
        return total

    zero = jnp.zeros((TILE, 256), F32)

    def older(low, high):
        def tile(i, carry):
            start = pl.multiple_of(i * TILE, TILE)
            rows = pl.ds(start, TILE)
            acc[rows, :] = attend(start, low, high, acc[rows, :])
            return carry

        lax.fori_loop(0, low // TILE, tile, 0)

    def newer(low, high):
        def tile(i, carry):
            start = pl.multiple_of(i * TILE, TILE)
            acc[pl.ds(start, TILE), :] = attend(start, 0, high, zero)
            return carry

        lax.fori_loop(low // TILE, high // TILE, tile, 0)

    def place(i):
        if i % 2:
            return lax.rem(z - (i + 1) // 2 * sign + RING, RING)
        return lax.rem(z + i // 2 * sign + RING, RING)

    def result_copy(t, i, side):
        target = {"seq": place(i), "cfg": c if side == 0 else other}
        return remote(
            ob.at[t, 2 * i + side],
            att.at[t, c, z],
            a2a_send.at[t, 2 * i + side],
            a2a_recv.at[t, mine],
            target,
        )

    def gather_and_attend(t):
        ring(t, slot(z, other), maj_send.at[t, 0], z_major).wait_recv()
        project(t, 0, [mine, slot(z, other)])
        newer(0, TILE)
        for i in range(1, 5):
            behind = lax.rem(z - i * sign + RING, RING)
            ahead = lax.rem(z + i * sign + RING, RING)
            ring(t, slot(behind, c), maj_send.at[t, 0], z_major).wait_recv()
            if i < 4:
                ring(t, slot(behind, c), maj_send.at[t, i], z_major).start()
            across(t, slot(behind, c), i).start()
            if i < 4:
                ring(t, slot(ahead, c), min_send.at[t, 0], z_minor).wait_recv()
                if i < 3:
                    ring(t, slot(ahead, c), min_send.at[t, i], z_minor).start()
                across(t, slot(ahead, c), 4 + i).start()
            across(t, slot(behind, other), 0).wait_recv()
            slots = [slot(behind, c), slot(behind, other)]
            if i < 4:
                across(t, slot(ahead, other), 0).wait_recv()
                slots += [slot(ahead, c), slot(ahead, other)]
            low = TILE + 2 * TILE * (i - 1)
            high = low + len(slots) * CHUNK
            project(t, low, slots)
            if i < 4:
                older(low, high)
                newer(low, high)
        last = FRAMES - TILE
        for i in (5, 6, 3, 4, 1, 2, 7, 0):
            if i == 7:
                total = attend(last, 0, FRAMES, zero)
            else:
                total = attend(i * TILE, last, FRAMES, acc[i * TILE : (i + 1) * TILE, :])
            result = (total[:, :128] / total[:, 128:]).astype(BF16)
            for side in range(2):
                piece = result[side * CHUNK : (side + 1) * CHUNK]
                if i == 0 and side == 0:
                    att[t, c, z] = piece
                else:
                    ob[t, 2 * i + side] = piece
                    result_copy(t, i, side).start()

    def clip_rows():
        return clip_ref[pl.ds(pl.multiple_of(c * CHUNK + k * 8, 8), 8), :]

    def peer_copy(src, dst, send, recv, t, o):
        target = lax.rem(k + o, STEPS)
        return remote(
            src.at[t, target], dst.at[t, k], send.at[t, o], recv.at[t, k], {"step": target}
        )

    def exchange(src, dst, send, recv, t):
        def start(o, carry):
            peer_copy(src, dst, send, recv, t, o).start()
            return carry

        lax.fori_loop(1, STEPS, start, 0)
        dst[t, k] = src[t, k]

        def arrive(o, carry):
            source = lax.rem(k + o, STEPS)
            remote(
                src.at[t, source],
                dst.at[t, source],
                send.at[t, o],
                recv.at[t, source],
                {"step": source},
            ).wait_recv()
            return carry

        lax.fori_loop(1, STEPS, arrive, 0)

    def merge(t):
        def arrive(o, carry):
            e = lax.rem(mine + o, COLUMN)
            zz, cc = e // 2, lax.rem(e, 2)
            remote(
                ob.at[t, 0],
                att.at[t, cc, zz],
                a2a_send.at[t, 0],
                a2a_recv.at[t, e],
                {"seq": zz, "cfg": cc},
            ).wait_recv()
            return carry

        lax.fori_loop(1, COLUMN, arrive, 0)
        attended = jnp.concatenate(
            [
                jnp.concatenate([att[t, cc, zz] for zz in range(RING)], axis=1)
                for cc in range(2)
            ],
            axis=0,
        )
        projected = jnp.dot(attended, w_out[...], preferred_element_type=F32)
        terms = projected[:CHUNK] * gates[0, :1, :] + projected[CHUNK:] * gates[1, :1, :]
        sb[t] = fold(terms.reshape(STEPS, 8, WIDTH))
        exchange(sb, rb, s_send, s_recv, t)
        return unfold(rb[t])

    def increment(j):
        return jnp.concatenate([incs[j]] * (WIDTH // 128), axis=1)

    gather_and_attend(0)
    loads[3].wait()
    gate_copy_back = remote(
        gates.at[other], gates.at[other], pair_send.at[0], pair_recv.at[0], {"cfg": other}
    )
    gate_copy_back.wait_recv()

    def inc_arrive(o, carry):
        source = lax.rem(k + o, STEPS)
        remote(
            incs.at[source],
            incs.at[source],
            inc_send.at[o],
            inc_recv.at[source],
            {"step": source},
        ).wait_recv()
        return carry

    lax.fori_loop(1, STEPS, inc_arrive, 0)

    terms = merge(0)
    start_rows = clip_rows()
    total = jnp.zeros_like(start_rows)
    for j in range(STEPS):
        states[j] = start_rows + total
        total = total + (increment(j) * start_rows + terms[j])
    nb[0] = fold(layer_norm(states[...]))
    exchange(nb, nr, n_send, n_recv, 0)
    xall[1, mine] = unfold(nr[0]).reshape(CHUNK, WIDTH).astype(BF16)

    begin(1)
    gather_and_attend(1)
    terms = merge(1)
    total = jnp.zeros_like(start_rows)
    drifts = []
    for j in range(STEPS):
        total = total + (increment(j) * states[j] + terms[j])
        drifts.append(total)
    nb[1] = fold(jnp.stack(drifts, axis=0))
    exchange(nb, nr, n_send, n_recv, 1)
    final_copy = remote(nr.at[1], fin, pair_send.at[1], pair_recv.at[1], {"cfg": other})
    final_copy.start()
    out_ref[own_rows, :] = clip_ref[own_rows, :] + unfold(nr[1]).reshape(CHUNK, WIDTH)
    final_copy.wait_recv()
    far_rows = pl.ds(pl.multiple_of(other * CHUNK, CHUNK), CHUNK)
    out_ref[far_rows, :] = clip_ref[far_rows, :] + unfold(fin[...]).reshape(CHUNK, WIDTH)

    final_copy.wait_send()
    gate_copy.wait_send()

    def inc_left(o, carry):
        inc_copy(o).wait_send()
        for t in range(2):
            peer_copy(sb, rb, s_send, s_recv, t, o).wait_send()
            peer_copy(nb, nr, n_send, n_recv, t, o).wait_send()
        return carry

    lax.fori_loop(1, STEPS, inc_left, 0)
    for t in range(2):
        for i in range(8):
            across(t, mine, i).wait_send()
            for side in range(2):
                if i or side:
                    result_copy(t, i, side).wait_send()
        for i in range(4):
            ring(t, mine, maj_send.at[t, i], z_major).wait_send()
        for i in range(3):
            ring(t, mine, min_send.at[t, i], z_minor).wait_send()


def local(clip, ordinal, strength, increment, table, pair, w_in, w_merge, sharp):
    vmem = pl.BlockSpec(memory_space=pltpu.VMEM)
    smem = pl.BlockSpec(memory_space=pltpu.SMEM)
    anywhere = pl.BlockSpec(memory_space=pl.ANY)
    dma = pltpu.SemaphoreType.DMA
    out = pl.pallas_call(
        kernel,
        out_shape=jax.ShapeDtypeStruct(clip.shape, F32),
        in_specs=[vmem, smem, smem, smem, vmem, vmem, anywhere, anywhere, smem],
        out_specs=vmem,
        scratch_shapes=[
            pltpu.VMEM((2, COLUMN, CHUNK, WIDTH), BF16),
            pltpu.VMEM((3, WIDTH, 128), BF16),
            pltpu.VMEM((WIDTH, 384), BF16),
            pltpu.VMEM((WIDTH, WIDTH), BF16),
            pltpu.VMEM((8, 384), F32),
            pltpu.VMEM((FRAMES, 128), BF16),
            pltpu.VMEM((2, FRAMES, 128), BF16),
            pltpu.VMEM((2, FRAMES, 256), BF16),
            pltpu.VMEM((FRAMES, 256), F32),
            pltpu.VMEM((2, COLUMN, CHUNK, 128), BF16),
            pltpu.VMEM((2, 2, RING, CHUNK, 128), BF16),
            pltpu.VMEM((2, STEPS, 16, 512), BF16),
            pltpu.VMEM((2, STEPS, 16, 512), BF16),
            pltpu.VMEM((2, STEPS, 16, 512), BF16),
            pltpu.VMEM((2, STEPS, 16, 512), BF16),
            pltpu.VMEM((STEPS, 16, 512), BF16),
            pltpu.VMEM((STEPS, 8, WIDTH), F32),
            pltpu.VMEM((2, 8, WIDTH), F32),
            pltpu.VMEM((STEPS, 8, 128), F32),
            dma((4,)),
            dma((2, 4)),
            dma((2, 3)),
            dma((2, 8)),
            dma((2, COLUMN)),
            dma((2, COLUMN)),
            dma((2, COLUMN)),
            dma((2, STEPS)),
            dma((2, STEPS)),
            dma((2, STEPS)),
            dma((2, STEPS)),
            dma((STEPS,)),
            dma((STEPS,)),
            dma((2,)),
            dma((2,)),
        ],
        compiler_params=pltpu.CompilerParams(
            collective_id=0, has_side_effects=True, vmem_limit_bytes=56 * 2**20
        ),
    )(clip, ordinal, strength, increment, table, pair, w_in, w_merge, sharp)
    return out[None]


def solution(mesh):
    placed = (P("seq", None), P("step"), P("step"), P("step"), P(), P("cfg", None), P(), P(), P())
    return jax.shard_map(
        local, mesh=mesh, in_specs=placed, out_specs=P("step", "seq", None), check_vma=False
    )
```

```python
import math

import jax
import jax.numpy as jnp
from jax import lax
from jax.experimental import pallas as pl
from jax.experimental.pallas import tpu as pltpu
from jax.sharding import PartitionSpec as P

MESH = pl.DeviceIdType.MESH
F32 = jnp.float32
BF16 = jnp.bfloat16
LOG2E = 1.4426950408889634

WIDTH = 1024
FRAMES = 2048
HALF = 64
CHUNK = 128
TILE = 256
RING = 8
STEPS = 16
COLUMN = 16


def remote(src, dst, send_sem, recv_sem, device):
    return pltpu.make_async_remote_copy(
        src_ref=src,
        dst_ref=dst,
        send_sem=send_sem,
        recv_sem=recv_sem,
        device_id=device,
        device_id_type=MESH,
    )


def fold(rows):
    half = WIDTH // 2
    return jnp.concatenate([rows[:, :, :half], rows[:, :, half:]], axis=1).astype(BF16)


def unfold(tiles):
    wide = tiles.astype(F32)
    return jnp.concatenate([wide[:, :8], wide[:, 8:]], axis=2)


def layer_norm(rows):
    average = jnp.mean(rows, axis=-1, keepdims=True)
    centred = rows - average
    variance = jnp.mean(centred * centred, axis=-1, keepdims=True)
    return centred * lax.rsqrt(variance + 1e-06)


def kernel(
    clip_ref,
    ordinal_ref,
    strength_ref,
    increment_ref,
    table_ref,
    pair_ref,
    w_in_ref,
    w_merge_ref,
    sharp_ref,
    out_ref,
    xall,
    w_raw,
    w_mod,
    w_out,
    bias,
    qb,
    kb,
    vb,
    acc,
    ob,
    att,
    sb,
    rb,
    nb,
    nr,
    fin,
    states,
    gates,
    incs,
    local_sem,
    maj_send,
    min_send,
    d2d_send,
    ring_recv,
    far_send,
    far_recv,
    plane_send,
    plane_recv,
    a2a_send,
    a2a_recv,
    s_send,
    s_recv,
    n_send,
    n_recv,
    inc_send,
    inc_recv,
    pair_send,
    pair_recv,
):
    k = lax.axis_index("step")
    c = lax.axis_index("cfg")
    z = lax.axis_index("seq")
    other = 1 - c
    sign = 1 - 2 * c
    mine = 2 * z + c

    barrier = pltpu.get_barrier_semaphore()

    def greet(o, carry):
        e = lax.rem(mine + o, COLUMN)
        pl.semaphore_signal(
            barrier, inc=1, device_id={"seq": e // 2, "cfg": lax.rem(e, 2)}, device_id_type=MESH
        )
        pl.semaphore_signal(
            barrier, inc=1, device_id={"step": lax.rem(k + o, STEPS)}, device_id_type=MESH
        )
        return carry

    lax.fori_loop(1, COLUMN, greet, 0)

    loads = []
    for part in range(3):
        columns = pl.ds(pl.multiple_of(part * WIDTH + z * 128, 128), 128)
        loads.append(
            pltpu.make_async_copy(
                w_in_ref.at[:, columns], w_raw.at[part], local_sem.at[part]
            )
        )
    loads.append(pltpu.make_async_copy(w_merge_ref, w_out, local_sem.at[3]))
    for load in loads:
        load.start()

    own_rows = pl.ds(pl.multiple_of(c * CHUNK, CHUNK), CHUNK)
    xall[0, 0, c] = layer_norm(clip_ref[own_rows, :]).astype(BF16)

    lane = lax.broadcasted_iota(jnp.int32, (1, 128), 1)
    first_head = lane < 64

    chosen = (
        lax.broadcasted_iota(jnp.int32, (16, table_ref.shape[0]), 1) == ordinal_ref[0]
    ).astype(BF16)
    affine = jnp.dot(chosen, table_ref[...], preferred_element_type=F32)[:8] + pair_ref[
        ...
    ].astype(F32)
    shift = affine[:, :WIDTH]
    scale_now = strength_ref[0]
    step_now = increment_ref[0]
    share = jnp.where(c == 0, scale_now, 1.0 - scale_now) * step_now
    gates[c] = affine[:, 2 * WIDTH :] * share
    incs[k] = jnp.full((8, 128), step_now, F32)
    scale_column = jnp.transpose(
        jnp.broadcast_to(1.0 + affine[:1, WIDTH : 2 * WIDTH], (128, WIDTH))
    )
    shift_high = shift.astype(BF16)
    shift_low = shift - shift_high.astype(F32)
    shift_parts = jnp.concatenate([shift_high.astype(F32), shift_low], axis=0).astype(BF16)
    for part in range(3):
        loads[part].wait()
        raw = w_raw[part]
        both = jnp.dot(shift_parts, raw, preferred_element_type=F32)
        bias[:, part * 128 : (part + 1) * 128] = both[:8] + both[8:]
        w_mod[:, part * 128 : (part + 1) * 128] = (raw.astype(F32) * scale_column).astype(BF16)
    ones = jnp.ones((1, 128), F32)
    for h in range(2):
        mask = first_head if h == 0 else jnp.logical_not(first_head)
        vb[h, :, 128:] = jnp.broadcast_to(jnp.where(mask, ones, 0.0), (FRAMES, 128)).astype(BF16)
    q_scale = jnp.where(first_head, sharp_ref[2 * z], sharp_ref[2 * z + 1]) * (
        LOG2E / math.sqrt(64.0)
    )
    same_head = (
        (lax.broadcasted_iota(jnp.int32, (128, 128), 0) < 64)
        == (lax.broadcasted_iota(jnp.int32, (128, 128), 1) < 64)
    ).astype(F32).astype(BF16)

    pl.semaphore_wait(barrier, 2 * (COLUMN - 1))

    def rel(offset):
        return lax.rem(offset * sign + RING, RING)

    def half_rows(h):
        return pl.ds(h * HALF, HALF)

    def at(t, offset, core, h):
        return xall.at[t, rel(offset), core, half_rows(h)]

    z_major = lax.rem(z + sign + RING, RING)
    z_minor = lax.rem(z - sign + RING, RING)

    def major(t, i, h):
        return remote(
            at(t, -i, c, h),
            at(t, -(i + 1), c, h),
            maj_send.at[t, i, h],
            ring_recv.at[t, rel(-(i + 1)), c, h],
            {"seq": z_major},
        )

    def minor(t, i, h):
        return remote(
            at(t, i, c, h),
            at(t, i + 1, c, h),
            min_send.at[t, i, h],
            ring_recv.at[t, rel(i + 1), c, h],
            {"seq": z_minor},
        )

    def across(t, offset, h, core):
        block = at(t, offset, core, h)
        return remote(
            block,
            block,
            d2d_send.at[t, rel(offset), h],
            ring_recv.at[t, rel(offset), core, h],
            {"cfg": other},
        )

    def begin(t):
        for h in range(2):
            major(t, 0, h).start()
            minor(t, 0, h).start()
        for h in range(2):
            across(t, 0, h, c).start()

    def onward(t, i, h, hops):
        major(t, i - 1, h).wait_recv()
        if i < hops:
            major(t, i, h).start()
        across(t, -i, h, c).start()
        if i < 4:
            minor(t, i - 1, h).wait_recv()
            if i < min(hops, 3):
                minor(t, i, h).start()
            across(t, i, h, c).start()

    def other_half_came(t, offset):
        for h in range(2):
            across(t, offset, h, other).wait_recv()

    piece = (
        pl.ds(pl.multiple_of(k // 8 * HALF, HALF), HALF),
        pl.ds(pl.multiple_of(lax.rem(k, 8) * 128, 128), 128),
    )

    def far_copy(i):
        return remote(
            xall.at[0, 0, c, piece[0], piece[1]],
            xall.at[0, 3 + i, c, piece[0], piece[1]],
            far_send.at[i],
            far_recv.at[i],
            {"seq": lax.rem(z + 5 - i, RING)},
        )

    def plane_block(step):
        return xall.at[
            0,
            pl.ds(3, 3),
            c,
            pl.ds(pl.multiple_of(step // 8 * HALF, HALF), HALF),
            pl.ds(pl.multiple_of(lax.rem(step, 8) * 128, 128), 128),
        ]

    def plane_copy(o):
        return remote(
            plane_block(k),
            plane_block(k),
            plane_send.at[o],
            plane_recv.at[k],
            {"step": lax.rem(k + o, STEPS)},
        )

    def plane_half(core, h):
        return xall.at[0, pl.ds(3, 3), core, half_rows(h)]

    def plane_across(core, h):
        block = plane_half(core, h)
        return remote(block, block, far_send.at[3 + h], far_recv.at[3 + h], {"cfg": other})

    begin(0)
    for i in range(3):
        far_copy(i).start()
    gate_copy = remote(
        gates.at[c], gates.at[c], pair_send.at[0], pair_recv.at[0], {"cfg": other}
    )
    gate_copy.start()

    def inc_copy(o):
        return remote(
            incs.at[k],
            incs.at[k],
            inc_send.at[o],
            inc_recv.at[k],
            {"step": lax.rem(k + o, STEPS)},
        )

    def send_inc(o, carry):
        inc_copy(o).start()
        return carry

    def project(t, start, slots):
        rows = len(slots) * CHUNK
        block = jnp.concatenate([xall[t, slab, core] for slab, core in slots], axis=0)
        qkv = jnp.dot(block, w_mod[...], preferred_element_type=F32) + bias[:1, :]
        here = pl.ds(start, rows)

        def normalize(values):
            squares = jnp.dot(
                (values * values).astype(BF16), same_head, preferred_element_type=F32
            )
            return values * lax.rsqrt(squares * (1.0 / 64.0) + 1e-06)

        qb[here, :] = (normalize(qkv[:, :128]) * q_scale).astype(BF16)
        keys = normalize(qkv[:, 128:256])
        values = qkv[:, 256:]
        for h in range(2):
            mask = first_head if h == 0 else jnp.logical_not(first_head)
            kb[h, here, :] = jnp.where(mask, keys, 0.0).astype(BF16)
            vb[h, here, :128] = jnp.where(mask, values, 0.0).astype(BF16)

    def attend(q_start, low, high, total):
        q = qb[pl.ds(q_start, TILE), :]
        for j in range(low, high, 256):
            for h in range(2):
                scores = lax.dot_general(
                    q, kb[h, j : j + 256, :], (((1,), (1,)), ((), ())), preferred_element_type=F32
                )
                powers = jnp.exp2(scores).astype(BF16)
                total = total + jnp.dot(
                    powers, vb[h, j : j + 256, :], preferred_element_type=F32
                )
        return total

    zero = jnp.zeros((TILE, 256), F32)

    def older(low, high):
        def tile(i, carry):
            start = pl.multiple_of(i * TILE, TILE)
            rows = pl.ds(start, TILE)
            acc[rows, :] = attend(start, low, high, acc[rows, :])
            return carry

        lax.fori_loop(0, low // TILE, tile, 0)

    def newer(low, high):
        def tile(i, carry):
            start = pl.multiple_of(i * TILE, TILE)
            acc[pl.ds(start, TILE), :] = attend(start, 0, high, zero)
            return carry

        lax.fori_loop(low // TILE, high // TILE, tile, 0)

    def place(t, i):
        if t == 0 and i in (3, 4, 5):
            return i
        if t == 0 and i > 5:
            i = i - 3
        return rel(-(i + 1) // 2 if i % 2 else i // 2)

    def result_copy(t, i, side):
        target = {"seq": lax.rem(z + place(t, i), RING), "cfg": c if side == 0 else other}
        return remote(
            ob.at[t, 2 * i + side],
            att.at[t, c, z],
            a2a_send.at[t, 2 * i + side],
            a2a_recv.at[t, mine],
            target,
        )

    def both(slab):
        return [(slab, c), (slab, other)]

    def gather_first():
        other_half_came(0, 0)
        project(0, 0, both(0))
        newer(0, TILE)
        for i in range(3):
            far_copy(i).wait_recv()

        def spread(o, carry):
            plane_copy(o).start()
            return carry

        lax.fori_loop(1, STEPS, spread, 0)
        lax.fori_loop(1, STEPS, send_inc, 0)
        onward(0, 1, 0, 2)
        onward(0, 1, 1, 2)
        other_half_came(0, -1)
        other_half_came(0, 1)
        project(0, 256, both(rel(-1)) + both(rel(1)))
        older(256, 768)
        onward(0, 2, 0, 2)
        newer(256, 768)

        def spread_came(o, carry):
            source = lax.rem(k + o, STEPS)
            block = plane_block(source)
            remote(
                block, block, plane_send.at[o], plane_recv.at[source], {"step": source}
            ).wait_recv()
            return carry

        lax.fori_loop(1, STEPS, spread_came, 0)
        for h in range(2):
            plane_across(c, h).start()
        onward(0, 2, 1, 2)
        for h in range(2):
            plane_across(other, h).wait_recv()
        project(0, 768, both(3) + both(4) + both(5))
        older(768, 1536)
        newer(768, 1536)
        other_half_came(0, -2)
        other_half_came(0, 2)
        project(0, 1536, both(rel(-2)) + both(rel(2)))
        finish(0, 1536, (4, 3, 5, 1, 2, 6, 7, 0))

    def gather_second():
        other_half_came(1, 0)
        project(1, 0, both(0))
        newer(0, TILE)
        onward(1, 1, 0, 4)
        for i in range(1, 5):
            onward(1, i, 1, 4)
            other_half_came(1, -i)
            slots = both(rel(-i))
            if i < 4:
                other_half_came(1, i)
                slots = slots + both(rel(i))
            low = TILE + 2 * TILE * (i - 1)
            high = low + len(slots) * CHUNK
            project(1, low, slots)
            if i < 4:
                older(low, high)
                onward(1, i + 1, 0, 4)
                newer(low, high)
        finish(1, FRAMES - TILE, (5, 6, 3, 4, 1, 2, 7, 0))

    def finish(t, last, order):
        for i in order:
            if i * TILE >= last:
                total = attend(i * TILE, 0, FRAMES, zero)
            else:
                total = attend(i * TILE, last, FRAMES, acc[i * TILE : (i + 1) * TILE, :])
            result = (total[:, :128] / total[:, 128:]).astype(BF16)
            for side in range(2):
                piece = result[side * CHUNK : (side + 1) * CHUNK]
                if i == 0 and side == 0:
                    att[t, c, z] = piece
                else:
                    ob[t, 2 * i + side] = piece
                    result_copy(t, i, side).start()

    def clip_rows():
        return clip_ref[pl.ds(pl.multiple_of(c * CHUNK + k * 8, 8), 8), :]

    def peer_copy(src, dst, send, recv, t, o):
        target = lax.rem(k + o, STEPS)
        return remote(
            src.at[t, target], dst.at[t, k], send.at[t, o], recv.at[t, k], {"step": target}
        )

    def exchange(src, dst, send, recv, t):
        def start(o, carry):
            peer_copy(src, dst, send, recv, t, o).start()
            return carry

        lax.fori_loop(1, STEPS, start, 0)
        dst[t, k] = src[t, k]

        def arrive(o, carry):
            source = lax.rem(k + o, STEPS)
            remote(
                src.at[t, source],
                dst.at[t, source],
                send.at[t, o],
                recv.at[t, source],
                {"step": source},
            ).wait_recv()
            return carry

        lax.fori_loop(1, STEPS, arrive, 0)

    def merge(t):
        def arrive(o, carry):
            e = lax.rem(mine + o, COLUMN)
            zz, cc = e // 2, lax.rem(e, 2)
            remote(
                ob.at[t, 0],
                att.at[t, cc, zz],
                a2a_send.at[t, 0],
                a2a_recv.at[t, e],
                {"seq": zz, "cfg": cc},
            ).wait_recv()
            return carry

        lax.fori_loop(1, COLUMN, arrive, 0)
        attended = jnp.concatenate(
            [
                jnp.concatenate([att[t, cc, zz] for zz in range(RING)], axis=1)
                for cc in range(2)
            ],
            axis=0,
        )
        projected = jnp.dot(attended, w_out[...], preferred_element_type=F32)
        terms = projected[:CHUNK] * gates[0, :1, :] + projected[CHUNK:] * gates[1, :1, :]
        sb[t] = fold(terms.reshape(STEPS, 8, WIDTH))
        exchange(sb, rb, s_send, s_recv, t)
        return unfold(rb[t])

    def increment(j):
        return jnp.concatenate([incs[j]] * (WIDTH // 128), axis=1)

    gather_first()
    loads[3].wait()
    gate_copy_back = remote(
        gates.at[other], gates.at[other], pair_send.at[0], pair_recv.at[0], {"cfg": other}
    )
    gate_copy_back.wait_recv()

    def inc_arrive(o, carry):
        source = lax.rem(k + o, STEPS)
        remote(
            incs.at[source],
            incs.at[source],
            inc_send.at[o],
            inc_recv.at[source],
            {"step": source},
        ).wait_recv()
        return carry

    lax.fori_loop(1, STEPS, inc_arrive, 0)

    terms = merge(0)
    start_rows = clip_rows()
    total = jnp.zeros_like(start_rows)
    for j in range(STEPS):
        states[j] = start_rows + total
        total = total + (increment(j) * start_rows + terms[j])
    nb[0] = fold(layer_norm(states[...]))
    exchange(nb, nr, n_send, n_recv, 0)
    xall[1, 0, c] = unfold(nr[0]).reshape(CHUNK, WIDTH).astype(BF16)

    begin(1)
    gather_second()
    terms = merge(1)
    total = jnp.zeros_like(start_rows)
    drifts = []
    for j in range(STEPS):
        total = total + (increment(j) * states[j] + terms[j])
        drifts.append(total)
    nb[1] = fold(jnp.stack(drifts, axis=0))
    exchange(nb, nr, n_send, n_recv, 1)
    final_copy = remote(nr.at[1], fin, pair_send.at[1], pair_recv.at[1], {"cfg": other})
    final_copy.start()
    out_ref[own_rows, :] = clip_ref[own_rows, :] + unfold(nr[1]).reshape(CHUNK, WIDTH)
    final_copy.wait_recv()
    far_rows = pl.ds(pl.multiple_of(other * CHUNK, CHUNK), CHUNK)
    out_ref[far_rows, :] = clip_ref[far_rows, :] + unfold(fin[...]).reshape(CHUNK, WIDTH)

    final_copy.wait_send()
    gate_copy.wait_send()

    def inc_left(o, carry):
        inc_copy(o).wait_send()
        for t in range(2):
            peer_copy(sb, rb, s_send, s_recv, t, o).wait_send()
            peer_copy(nb, nr, n_send, n_recv, t, o).wait_send()
        return carry

    lax.fori_loop(1, STEPS, inc_left, 0)
    for i in range(3):
        far_copy(i).wait_send()
    for h in range(2):
        plane_across(c, h).wait_send()

    def plane_left(o, carry):
        plane_copy(o).wait_send()
        return carry

    lax.fori_loop(1, STEPS, plane_left, 0)
    for t in range(2):
        for i in range(8):
            for side in range(2):
                if i or side:
                    result_copy(t, i, side).wait_send()
        hops = (2, 4)[t]
        for h in range(2):
            across(t, 0, h, c).wait_send()
            for i in range(hops):
                major(t, i, h).wait_send()
                across(t, -(i + 1), h, c).wait_send()
            for i in range(min(hops, 3)):
                minor(t, i, h).wait_send()
                across(t, i + 1, h, c).wait_send()


def local(clip, ordinal, strength, increment, table, pair, w_in, w_merge, sharp):
    vmem = pl.BlockSpec(memory_space=pltpu.VMEM)
    smem = pl.BlockSpec(memory_space=pltpu.SMEM)
    anywhere = pl.BlockSpec(memory_space=pl.ANY)
    dma = pltpu.SemaphoreType.DMA
    out = pl.pallas_call(
        kernel,
        out_shape=jax.ShapeDtypeStruct(clip.shape, F32),
        in_specs=[vmem, smem, smem, smem, vmem, vmem, anywhere, anywhere, smem],
        out_specs=vmem,
        scratch_shapes=[
            pltpu.VMEM((2, RING, 2, CHUNK, WIDTH), BF16),
            pltpu.VMEM((3, WIDTH, 128), BF16),
            pltpu.VMEM((WIDTH, 384), BF16),
            pltpu.VMEM((WIDTH, WIDTH), BF16),
            pltpu.VMEM((8, 384), F32),
            pltpu.VMEM((FRAMES, 128), BF16),
            pltpu.VMEM((2, FRAMES, 128), BF16),
            pltpu.VMEM((2, FRAMES, 256), BF16),
            pltpu.VMEM((FRAMES, 256), F32),
            pltpu.VMEM((2, COLUMN, CHUNK, 128), BF16),
            pltpu.VMEM((2, 2, RING, CHUNK, 128), BF16),
            pltpu.VMEM((2, STEPS, 16, 512), BF16),
            pltpu.VMEM((2, STEPS, 16, 512), BF16),
            pltpu.VMEM((2, STEPS, 16, 512), BF16),
            pltpu.VMEM((2, STEPS, 16, 512), BF16),
            pltpu.VMEM((STEPS, 16, 512), BF16),
            pltpu.VMEM((STEPS, 8, WIDTH), F32),
            pltpu.VMEM((2, 8, WIDTH), F32),
            pltpu.VMEM((STEPS, 8, 128), F32),
            dma((4,)),
            dma((2, 4, 2)),
            dma((2, 3, 2)),
            dma((2, RING, 2)),
            dma((2, RING, 2, 2)),
            dma((5,)),
            dma((5,)),
            dma((STEPS,)),
            dma((STEPS,)),
            dma((2, COLUMN)),
            dma((2, COLUMN)),
            dma((2, STEPS)),
            dma((2, STEPS)),
            dma((2, STEPS)),
            dma((2, STEPS)),
            dma((STEPS,)),
            dma((STEPS,)),
            dma((2,)),
            dma((2,)),
        ],
        compiler_params=pltpu.CompilerParams(
            collective_id=0, has_side_effects=True, vmem_limit_bytes=56 * 2**20
        ),
    )(clip, ordinal, strength, increment, table, pair, w_in, w_merge, sharp)
    return out[None]


def solution(mesh):
    placed = (P("seq", None), P("step"), P("step"), P("step"), P(), P("cfg", None), P(), P(), P())
    return jax.shard_map(
        local, mesh=mesh, in_specs=placed, out_specs=P("step", "seq", None), check_vma=False
    )
```

```python
import math

import jax
import jax.numpy as jnp
from jax import lax
from jax.experimental import pallas as pl
from jax.experimental.pallas import tpu as pltpu
from jax.sharding import PartitionSpec as P

MESH = pl.DeviceIdType.MESH
F32 = jnp.float32
BF16 = jnp.bfloat16
LOG2E = 1.4426950408889634

WIDTH = 1024
FRAMES = 2048
HALF = 64
CHUNK = 128
TILE = 256
RING = 8
STEPS = 16
COLUMN = 16


def remote(src, dst, send_sem, recv_sem, device):
    return pltpu.make_async_remote_copy(
        src_ref=src,
        dst_ref=dst,
        send_sem=send_sem,
        recv_sem=recv_sem,
        device_id=device,
        device_id_type=MESH,
    )


def fold(rows):
    half = WIDTH // 2
    return jnp.concatenate([rows[:, :, :half], rows[:, :, half:]], axis=1).astype(BF16)


def unfold(tiles):
    wide = tiles.astype(F32)
    return jnp.concatenate([wide[:, :8], wide[:, 8:]], axis=2)


def layer_norm(rows):
    average = jnp.mean(rows, axis=-1, keepdims=True)
    centred = rows - average
    variance = jnp.mean(centred * centred, axis=-1, keepdims=True)
    return centred * lax.rsqrt(variance + 1e-06)


def kernel(
    clip_ref,
    ordinal_ref,
    strength_ref,
    increment_ref,
    table_ref,
    pair_ref,
    w_in_ref,
    w_merge_ref,
    sharp_ref,
    out_ref,
    xall,
    w_raw,
    w_mod,
    w_out,
    bias,
    qb,
    kb,
    vt,
    acc,
    ob,
    att,
    sb,
    rb,
    nb,
    nr,
    fin,
    states,
    gates,
    incs,
    out_rows,
    local_sem,
    maj_send,
    min_send,
    d2d_send,
    ring_recv,
    far_send,
    far_recv,
    plane_send,
    plane_recv,
    a2a_send,
    a2a_recv,
    s_send,
    s_recv,
    n_send,
    n_recv,
    inc_send,
    inc_recv,
    pair_send,
    pair_recv,
):
    k = lax.axis_index("step")
    c = lax.axis_index("cfg")
    z = lax.axis_index("seq")
    other = 1 - c
    sign = 1 - 2 * c
    mine = 2 * z + c

    barrier = pltpu.get_barrier_semaphore()

    def greet(o, carry):
        e = lax.rem(mine + o, COLUMN)
        pl.semaphore_signal(
            barrier, inc=1, device_id={"seq": e // 2, "cfg": lax.rem(e, 2)}, device_id_type=MESH
        )
        pl.semaphore_signal(
            barrier, inc=1, device_id={"step": lax.rem(k + o, STEPS)}, device_id_type=MESH
        )
        return carry

    lax.fori_loop(1, COLUMN, greet, 0)

    loads = []
    for part in range(3):
        columns = pl.ds(pl.multiple_of(part * WIDTH + z * 128, 128), 128)
        loads.append(
            pltpu.make_async_copy(
                w_in_ref.at[:, columns], w_raw.at[part], local_sem.at[part]
            )
        )
    loads.append(pltpu.make_async_copy(w_merge_ref, w_out, local_sem.at[3]))
    for load in loads:
        load.start()

    own_rows = pl.ds(pl.multiple_of(c * CHUNK, CHUNK), CHUNK)
    xall[0, 0, c] = layer_norm(clip_ref[own_rows, :]).astype(BF16)

    lane = lax.broadcasted_iota(jnp.int32, (1, 128), 1)
    first_head = lane < 64

    chosen = (
        lax.broadcasted_iota(jnp.int32, (16, table_ref.shape[0]), 1) == ordinal_ref[0]
    ).astype(BF16)
    affine = jnp.dot(chosen, table_ref[...], preferred_element_type=F32)[:8] + pair_ref[
        ...
    ].astype(F32)
    shift = affine[:, :WIDTH]
    scale_now = strength_ref[0]
    step_now = increment_ref[0]
    share = jnp.where(c == 0, scale_now, 1.0 - scale_now) * step_now
    gates[c] = affine[:, 2 * WIDTH :] * share
    incs[k] = jnp.full((8, 128), step_now, F32)
    scale_column = jnp.transpose(
        jnp.broadcast_to(1.0 + affine[:1, WIDTH : 2 * WIDTH], (128, WIDTH))
    )
    shift_high = shift.astype(BF16)
    shift_low = shift - shift_high.astype(F32)
    shift_parts = jnp.concatenate([shift_high.astype(F32), shift_low], axis=0).astype(BF16)
    for part in range(3):
        loads[part].wait()
        raw = w_raw[part]
        both = jnp.dot(shift_parts, raw, preferred_element_type=F32)
        bias[:, part * 128 : (part + 1) * 128] = both[:8] + both[8:]
        w_mod[:, part * 128 : (part + 1) * 128] = (raw.astype(F32) * scale_column).astype(BF16)
    for h in range(2):
        vt[h, 64:, :] = jnp.ones((16, FRAMES), BF16)
    q_scale = jnp.where(first_head, sharp_ref[2 * z], sharp_ref[2 * z + 1]) * (
        LOG2E / math.sqrt(64.0)
    )
    same_head = (
        (lax.broadcasted_iota(jnp.int32, (128, 128), 0) < 64)
        == (lax.broadcasted_iota(jnp.int32, (128, 128), 1) < 64)
    ).astype(F32).astype(BF16)

    pl.semaphore_wait(barrier, 2 * (COLUMN - 1))

    def rel(offset):
        return lax.rem(offset * sign + RING, RING)

    def half_rows(h):
        return pl.ds(h * HALF, HALF)

    def at(t, offset, core, h):
        return xall.at[t, rel(offset), core, half_rows(h)]

    z_major = lax.rem(z + sign + RING, RING)
    z_minor = lax.rem(z - sign + RING, RING)

    def major(t, i, h):
        return remote(
            at(t, -i, c, h),
            at(t, -(i + 1), c, h),
            maj_send.at[t, i, h],
            ring_recv.at[t, rel(-(i + 1)), c, h],
            {"seq": z_major},
        )

    def minor(t, i, h):
        return remote(
            at(t, i, c, h),
            at(t, i + 1, c, h),
            min_send.at[t, i, h],
            ring_recv.at[t, rel(i + 1), c, h],
            {"seq": z_minor},
        )

    def across(t, offset, h, core):
        block = at(t, offset, core, h)
        return remote(
            block,
            block,
            d2d_send.at[t, rel(offset), h],
            ring_recv.at[t, rel(offset), core, h],
            {"cfg": other},
        )

    def begin(t, h):
        major(t, 0, h).start()
        minor(t, 0, h).start()
        across(t, 0, h, c).start()

    def onward(t, i, h, hops):
        major(t, i - 1, h).wait_recv()
        if i < hops:
            major(t, i, h).start()
        across(t, -i, h, c).start()
        if i < 4:
            minor(t, i - 1, h).wait_recv()
            if i < min(hops, 3):
                minor(t, i, h).start()
            across(t, i, h, c).start()

    def other_half_came(t, offset):
        for h in range(2):
            across(t, offset, h, other).wait_recv()

    x, y = lax.rem(k, 4), k // 4
    one, two = x + c * (y - x), y + c * (x - y)
    step_one, step_two = 1 + 3 * c, 4 - 3 * c

    def piece_rows(index):
        return pl.ds(pl.multiple_of(index * 32, 32), 32)

    def piece_lanes(index):
        return pl.ds(pl.multiple_of(index * 256, 256), 256)

    def far_copy(i):
        return remote(
            xall.at[0, 0, c, piece_rows(two), piece_lanes(one)],
            xall.at[0, 3 + i, c, piece_rows(two), piece_lanes(one)],
            far_send.at[i],
            far_recv.at[i],
            {"seq": lax.rem(z + 5 - i, RING)},
        )

    def plane_one(o, came=False):
        peer = lax.rem(one + o, 4)
        block = xall.at[
            0, pl.ds(3, 3), c, piece_rows(two), piece_lanes(peer if came else one)
        ]
        return remote(
            block,
            block,
            plane_send.at[0, o],
            plane_recv.at[0, peer if came else one],
            {"step": k + (peer - one) * step_one},
        )

    def plane_two(o, came=False):
        peer = lax.rem(two + o, 4)
        block = xall.at[0, pl.ds(3, 3), c, piece_rows(peer if came else two)]
        return remote(
            block,
            block,
            plane_send.at[1, o],
            plane_recv.at[1, peer if came else two],
            {"step": k + (peer - two) * step_two},
        )

    def plane_half(core, h):
        return xall.at[0, pl.ds(3, 3), core, half_rows(h)]

    def plane_across(core, h):
        block = plane_half(core, h)
        return remote(block, block, far_send.at[3 + h], far_recv.at[3 + h], {"cfg": other})

    for i in range(3):
        far_copy(i).start()
    for h in range(2):
        begin(0, h)
    gate_copy = remote(
        gates.at[c], gates.at[c], pair_send.at[0], pair_recv.at[0], {"cfg": other}
    )
    gate_copy.start()

    def inc_copy(o):
        return remote(
            incs.at[k],
            incs.at[k],
            inc_send.at[o],
            inc_recv.at[k],
            {"step": lax.rem(k + o, STEPS)},
        )

    def send_inc(o, carry):
        inc_copy(o).start()
        return carry

    def project(t, start, slots):
        rows = len(slots) * CHUNK
        block = jnp.concatenate([xall[t, slab, core] for slab, core in slots], axis=0)
        qkv = jnp.dot(block, w_mod[...], preferred_element_type=F32) + bias[:1, :]
        here = pl.ds(start, rows)

        def normalize(values):
            squares = jnp.dot(
                (values * values).astype(BF16), same_head, preferred_element_type=F32
            )
            return values * lax.rsqrt(squares * (1.0 / 64.0) + 1e-06)

        queries = normalize(qkv[:, :128]) * q_scale
        for i in range(0, rows, TILE):
            parts = [queries[i + r : i + r + HALF] for r in (0, CHUNK, HALF, CHUNK + HALF)]
            qb[pl.ds(start + i, TILE), :] = jnp.concatenate(parts, axis=0).astype(BF16)
        keys = normalize(qkv[:, 128:256])
        values = jnp.transpose(qkv[:, 256:])
        for h in range(2):
            mask = first_head if h == 0 else jnp.logical_not(first_head)
            kb[h, here, :] = jnp.where(mask, keys, 0.0).astype(BF16)
            vt[h, :64, here] = values[h * 64 : (h + 1) * 64].astype(BF16)

    def attend(q, low, high, totals):
        totals = list(totals)
        for j in range(low, high, 1024):
            end = min(j + 1024, high)
            for h in range(2):
                scores = lax.dot_general(
                    kb[h, j:end, :], q, (((1,), (1,)), ((), ())), preferred_element_type=F32
                )
                powers = jnp.exp2(scores).astype(BF16)
                totals[h] = totals[h] + jnp.dot(
                    vt[h, :, j:end], powers, preferred_element_type=F32
                )
        return totals

    def zeros(count):
        return [jnp.zeros((80, count), F32)] * 2

    def pieces(low, high):
        count = -(-(high - low) // 1024)
        each = (high - low) // count
        return [(low + n * each, low + (n + 1) * each) for n in range(count)]

    def older(low, high):
        for a, b in pieces(0, low):
            totals = attend(qb[a:b, :], low, high, [acc[0, :, a:b], acc[1, :, a:b]])
            for h in range(2):
                acc[h, :, a:b] = totals[h]

    def newer(low, high, last):
        for a, b in pieces(low, high):
            totals = attend(qb[a:b, :], 0, last, zeros(b - a))
            for h in range(2):
                acc[h, :, a:b] = totals[h]

    def place(t, i):
        if t == 0 and i > 4:
            return i - 2
        return rel(-(i + 1) // 2 if i % 2 else i // 2)

    def result_copy(t, h, i, side):
        target = {"seq": lax.rem(z + place(t, i), RING), "cfg": c if side == 0 else other}
        return remote(
            ob.at[t, h, 2 * i + side],
            att.at[t, h, c, z],
            a2a_send.at[t, h, 2 * i + side],
            a2a_recv.at[t, h, mine],
            target,
        )

    def both(slab):
        return [(slab, c), (slab, other)]

    def gather_first():
        other_half_came(0, 0)
        project(0, 0, both(0))
        newer(0, TILE, TILE)
        for i in range(3):
            far_copy(i).wait_recv()
        for o in (2, 1, 3):
            plane_one(o).start()
        lax.fori_loop(1, STEPS, send_inc, 0)
        onward(0, 1, 0, 2)
        onward(0, 1, 1, 2)
        other_half_came(0, -1)
        other_half_came(0, 1)
        project(0, 256, both(rel(-1)) + both(rel(1)))
        older(256, 768)
        for o in (1, 3, 2):
            plane_one(o, came=True).wait_recv()
        for o in (2, 1, 3):
            plane_two(o).start()
        newer(256, 768, 768)
        onward(0, 2, 0, 2)
        onward(0, 2, 1, 2)
        other_half_came(0, -2)
        other_half_came(0, 2)
        project(0, 768, both(rel(-2)) + both(rel(2)))
        older(768, 1280)
        for o in (1, 3, 2):
            plane_two(o, came=True).wait_recv()
        for h in range(2):
            plane_across(c, h).start()
        newer(768, 1280, 1280)
        for h in range(2):
            plane_across(other, h).wait_recv()
        project(0, 1280, both(3) + both(4) + both(5))
        finish(0, 1280, (6, 5, 7, 3, 4, 1, 2, 0))

    def gather_second():
        other_half_came(1, 0)
        project(1, 0, both(0))
        newer(0, TILE, TILE)
        onward(1, 2, 0, 4)
        for i in range(1, 5):
            onward(1, i, 1, 4)
            other_half_came(1, -i)
            slots = both(rel(-i))
            if i < 4:
                other_half_came(1, i)
                slots = slots + both(rel(i))
            low = TILE + 2 * TILE * (i - 1)
            high = low + len(slots) * CHUNK
            project(1, low, slots)
            if i < 4:
                older(low, high)
                if i < 3:
                    onward(1, i + 2, 0, 4)
                newer(low, high, high)
        finish(1, FRAMES - TILE, (7, 5, 6, 3, 4, 1, 2, 0))

    def each_result(t, h, order, act):
        for i in order:
            for side in range(2):
                if i or side:
                    act(result_copy(t, h, i, side))

    def finish(t, last, order):
        newer(last, FRAMES, last)
        for half in range(2):
            starts = [i * TILE + half * CHUNK for i in order]
            totals = attend(
                jnp.concatenate([qb[r : r + CHUNK, :] for r in starts], axis=0),
                last,
                FRAMES,
                [
                    jnp.concatenate([acc[h, :, r : r + CHUNK] for r in starts], axis=1)
                    for h in range(2)
                ],
            )
            result = jnp.transpose(
                jnp.concatenate([a[:64] * (1.0 / a[64:65]) for a in totals], axis=0)
            ).astype(BF16)
            for n, i in enumerate(order):
                for side in range(2):
                    start = n * CHUNK + side * HALF
                    piece = result[start : start + HALF]
                    if i == 0 and side == 0:
                        att[t, half, c, z] = piece
                    else:
                        ob[t, half, 2 * i + side] = piece
            each_result(t, half, order, lambda copy: copy.start())

    colour = lax.rem(x + y, 2)

    def owner(spot, h):
        return 2 * spot + lax.rem(spot // 2 + h, 2)

    def clip_rows():
        start = c * CHUNK + colour * HALF + k // 2 * 8
        return clip_ref[pl.ds(pl.multiple_of(start, 8), 8), :]

    def term_copy(t, h, j):
        spot = lax.rem(j + k // 2, 8)
        return remote(
            sb.at[t, h, spot],
            rb.at[t, k],
            s_send.at[t, h, spot],
            s_recv.at[t, k],
            {"step": owner(spot, h)},
        )

    def each_owner(t, h, act):
        def one_owner(j, carry):
            @pl.when(owner(lax.rem(j + k // 2, 8), h) != k)
            def _():
                act(term_copy(t, h, j))

            return carry

        lax.fori_loop(0, 8, one_owner, 0)

    def back_copy(t, o):
        target = lax.rem(k + o, STEPS)
        return remote(
            nb.at[t, target],
            nr.at[t, colour, k // 2],
            n_send.at[t, o],
            n_recv.at[t, k],
            {"step": target},
        )

    def merge(t, h):
        def arrive(o, carry):
            e = lax.rem(mine + o, COLUMN)
            zz, cc = e // 2, lax.rem(e, 2)
            remote(
                ob.at[t, h, 0],
                att.at[t, h, cc, zz],
                a2a_send.at[t, h, 0],
                a2a_recv.at[t, h, e],
                {"seq": zz, "cfg": cc},
            ).wait_recv()
            return carry

        lax.fori_loop(1, COLUMN, arrive, 0)
        attended = jnp.concatenate(
            [
                jnp.concatenate([att[t, h, cc, zz] for zz in range(RING)], axis=1)
                for cc in range(2)
            ],
            axis=0,
        )
        projected = jnp.dot(attended, w_out[...], preferred_element_type=F32)
        terms = projected[:HALF] * gates[0, :1, :] + projected[HALF:] * gates[1, :1, :]
        sb[t, h] = fold(terms.reshape(8, 8, WIDTH))

    def send_terms(t, h):
        each_owner(t, h, lambda copy: copy.start())

    def own(t, h):
        @pl.when(colour == h)
        def _():
            rb[t, k] = sb[t, h, k // 2]

            def arrive(o, carry):
                source = lax.rem(k + o, STEPS)
                remote(
                    sb.at[t, 0, 0],
                    rb.at[t, source],
                    s_send.at[t, 0, 0],
                    s_recv.at[t, source],
                    {"step": source},
                ).wait_recv()
                return carry

            lax.fori_loop(1, STEPS, arrive, 0)
            terms = unfold(rb[t])
            start_rows = clip_rows()
            total = jnp.zeros_like(start_rows)
            if t == 0:
                for j in range(STEPS):
                    states[j] = start_rows + total
                    total = total + (increment(j) * start_rows + terms[j])
                nb[0] = fold(layer_norm(states[...]))
            else:
                drifts = []
                for j in range(STEPS):
                    total = total + (increment(j) * states[j] + terms[j])
                    drifts.append(total)
                nb[1] = fold(jnp.stack(drifts, axis=0))

            def back(o, carry):
                back_copy(t, o).start()
                return carry

            lax.fori_loop(1, STEPS, back, 0)
            nr[t, h, k // 2] = nb[t, k]

    def rows_back(t, h):
        def arrive(j, carry):
            source = owner(lax.rem(j + k // 2, 8), h)

            @pl.when(source != k)
            def _():
                remote(
                    nb.at[t, 0],
                    nr.at[t, h, source // 2],
                    n_send.at[t, 0],
                    n_recv.at[t, source],
                    {"step": source},
                ).wait_recv()

            return carry

        lax.fori_loop(0, 8, arrive, 0)
        return unfold(nr[t, h]).reshape(HALF, WIDTH)

    def next_rows(h):
        xall[1, 0, c, half_rows(h)] = rows_back(0, h).astype(BF16)
        begin(1, h)

    def final_copy(h):
        return remote(
            nr.at[1, h], fin.at[h], pair_send.at[1 + h], pair_recv.at[1 + h], {"cfg": other}
        )

    def out_copy(rows, i):
        return pltpu.make_async_copy(
            out_rows.at[rows], out_ref.at[rows], local_sem.at[4 + i]
        )

    def own_out(h):
        rows = pl.ds(pl.multiple_of(c * CHUNK + h * HALF, HALF), HALF)
        drift = rows_back(1, h)
        final_copy(h).start()
        out_rows[rows, :] = clip_ref[rows, :] + drift
        out_copy(rows, h).start()

    def increment(j):
        return jnp.concatenate([incs[j]] * (WIDTH // 128), axis=1)

    def ring_left(t):
        hops = (2, 4)[t]
        for h in range(2):
            across(t, 0, h, c).wait_send()
            for i in range(hops):
                major(t, i, h).wait_send()
                across(t, -(i + 1), h, c).wait_send()
            for i in range(min(hops, 3)):
                minor(t, i, h).wait_send()
                across(t, i + 1, h, c).wait_send()

    def exchange_left(t):
        def left(o, carry):
            back_copy(t, o).wait_send()
            return carry

        lax.fori_loop(1, STEPS, left, 0)
        for h in range(2):
            each_owner(t, h, lambda copy: copy.wait_send())

    def inc_left(o, carry):
        inc_copy(o).wait_send()
        return carry

    gather_first()
    loads[3].wait()
    gate_copy_back = remote(
        gates.at[other], gates.at[other], pair_send.at[0], pair_recv.at[0], {"cfg": other}
    )
    gate_copy_back.wait_recv()

    def inc_arrive(o, carry):
        source = lax.rem(k + o, STEPS)
        remote(
            incs.at[source],
            incs.at[source],
            inc_send.at[o],
            inc_recv.at[source],
            {"step": source},
        ).wait_recv()
        return carry

    lax.fori_loop(1, STEPS, inc_arrive, 0)

    merge(0, 0)
    send_terms(0, 0)
    own(0, 0)
    merge(0, 1)
    send_terms(0, 1)
    next_rows(0)
    own(0, 1)
    onward(1, 1, 0, 4)
    next_rows(1)

    gate_copy.wait_send()
    ring_left(0)
    exchange_left(0)
    for h in range(2):
        each_result(0, h, range(8), lambda copy: copy.wait_send())
    lax.fori_loop(1, STEPS, inc_left, 0)
    for i in range(3):
        far_copy(i).wait_send()
    for h in range(2):
        plane_across(c, h).wait_send()
    for o in range(1, 4):
        plane_one(o).wait_send()
        plane_two(o).wait_send()

    gather_second()
    ring_left(1)
    merge(1, 0)
    merge(1, 1)
    send_terms(1, 0)
    send_terms(1, 1)
    for h in range(2):
        each_result(1, h, range(8), lambda copy: copy.wait_send())
    for h in range(2):
        own(1, h)
    own_out(0)
    own_out(1)
    for h in range(2):
        rows = pl.ds(pl.multiple_of(other * CHUNK + h * HALF, HALF), HALF)
        final_copy(h).wait_recv()
        out_rows[rows, :] = clip_ref[rows, :] + unfold(fin[h]).reshape(HALF, WIDTH)
        out_copy(rows, 2 + h).start()
    exchange_left(1)
    for h in range(2):
        final_copy(h).wait_send()
        out_copy(half_rows(h), h).wait()
        out_copy(half_rows(h), 2 + h).wait()


def local(clip, ordinal, strength, increment, table, pair, w_in, w_merge, sharp):
    vmem = pl.BlockSpec(memory_space=pltpu.VMEM)
    smem = pl.BlockSpec(memory_space=pltpu.SMEM)
    anywhere = pl.BlockSpec(memory_space=pl.ANY)
    dma = pltpu.SemaphoreType.DMA
    out = pl.pallas_call(
        kernel,
        out_shape=jax.ShapeDtypeStruct(clip.shape, F32),
        in_specs=[vmem, smem, smem, smem, vmem, vmem, anywhere, anywhere, smem],
        out_specs=anywhere,
        scratch_shapes=[
            pltpu.VMEM((2, RING, 2, CHUNK, WIDTH), BF16),
            pltpu.VMEM((3, WIDTH, 128), BF16),
            pltpu.VMEM((WIDTH, 384), BF16),
            pltpu.VMEM((WIDTH, WIDTH), BF16),
            pltpu.VMEM((8, 384), F32),
            pltpu.VMEM((FRAMES, 128), BF16),
            pltpu.VMEM((2, FRAMES, 128), BF16),
            pltpu.VMEM((2, 80, FRAMES), BF16),
            pltpu.VMEM((2, 80, FRAMES), F32),
            pltpu.VMEM((2, 2, COLUMN, HALF, 128), BF16),
            pltpu.VMEM((2, 2, 2, RING, HALF, 128), BF16),
            pltpu.VMEM((2, 2, 8, 16, 512), BF16),
            pltpu.VMEM((2, STEPS, 16, 512), BF16),
            pltpu.VMEM((2, STEPS, 16, 512), BF16),
            pltpu.VMEM((2, 2, 8, 16, 512), BF16),
            pltpu.VMEM((2, 8, 16, 512), BF16),
            pltpu.VMEM((STEPS, 8, WIDTH), F32),
            pltpu.VMEM((2, 8, WIDTH), F32),
            pltpu.VMEM((STEPS, 8, 128), F32),
            pltpu.VMEM((2 * CHUNK, WIDTH), F32),
            dma((8,)),
            dma((2, 4, 2)),
            dma((2, 3, 2)),
            dma((2, RING, 2)),
            dma((2, RING, 2, 2)),
            dma((5,)),
            dma((5,)),
            dma((2, 4)),
            dma((2, 4)),
            dma((2, 2, COLUMN)),
            dma((2, 2, COLUMN)),
            dma((2, 2, 8)),
            dma((2, STEPS)),
            dma((2, STEPS)),
            dma((2, STEPS)),
            dma((STEPS,)),
            dma((STEPS,)),
            dma((3,)),
            dma((3,)),
        ],
        compiler_params=pltpu.CompilerParams(
            collective_id=0, has_side_effects=True, vmem_limit_bytes=56 * 2**20
        ),
    )(clip, ordinal, strength, increment, table, pair, w_in, w_merge, sharp)
    return out[None]


def solution(mesh):
    placed = (P("seq", None), P("step"), P("step"), P("step"), P(), P("cfg", None), P(), P(), P())
    return jax.shard_map(
        local, mesh=mesh, in_specs=placed, out_specs=P("step", "seq", None), check_vma=False
    )
```

```python
import math

import jax
import jax.numpy as jnp
from jax import lax
from jax.experimental import pallas as pl
from jax.experimental.pallas import tpu as pltpu
from jax.sharding import PartitionSpec as P

MESH = pl.DeviceIdType.MESH
F32 = jnp.float32
BF16 = jnp.bfloat16
LOG2E = 1.4426950408889634

WIDTH = 1024
FRAMES = 2048
HALF = 64
CHUNK = 128
TILE = 256
RING = 8
STEPS = 16
COLUMN = 16


def remote(src, dst, send_sem, recv_sem, device):
    return pltpu.make_async_remote_copy(
        src_ref=src,
        dst_ref=dst,
        send_sem=send_sem,
        recv_sem=recv_sem,
        device_id=device,
        device_id_type=MESH,
    )


def fold(rows):
    half = WIDTH // 2
    return jnp.concatenate([rows[:, :, :half], rows[:, :, half:]], axis=1).astype(BF16)


def unfold(tiles):
    wide = tiles.astype(F32)
    return jnp.concatenate([wide[:, :8], wide[:, 8:]], axis=2)


def layer_norm(rows):
    average = jnp.mean(rows, axis=-1, keepdims=True)
    centred = rows - average
    variance = jnp.mean(centred * centred, axis=-1, keepdims=True)
    return centred * lax.rsqrt(variance + 1e-06)


def kernel(
    clip_ref,
    ordinal_ref,
    strength_ref,
    increment_ref,
    table_ref,
    pair_ref,
    w_in_ref,
    w_merge_ref,
    sharp_ref,
    out_ref,
    xall,
    w_raw,
    w_mod,
    w_out,
    bias,
    qb,
    kb,
    vt,
    acc,
    ob,
    att,
    sb,
    rb,
    nb,
    nr,
    fin,
    states,
    gates,
    incs,
    out_rows,
    local_sem,
    maj_send,
    min_send,
    d2d_send,
    ring_recv,
    far_send,
    far_recv,
    plane_send,
    plane_recv,
    a2a_send,
    a2a_recv,
    s_send,
    s_recv,
    n_send,
    n_recv,
    inc_send,
    inc_recv,
    pair_send,
    pair_recv,
):
    k = lax.axis_index("step")
    c = lax.axis_index("cfg")
    z = lax.axis_index("seq")
    other = 1 - c
    sign = 1 - 2 * c
    mine = 2 * z + c

    barrier = pltpu.get_barrier_semaphore()

    def greet(o, carry):
        e = lax.rem(mine + o, COLUMN)
        pl.semaphore_signal(
            barrier, inc=1, device_id={"seq": e // 2, "cfg": lax.rem(e, 2)}, device_id_type=MESH
        )
        pl.semaphore_signal(
            barrier, inc=1, device_id={"step": lax.rem(k + o, STEPS)}, device_id_type=MESH
        )
        return carry

    lax.fori_loop(1, COLUMN, greet, 0)

    loads = []
    for part in range(3):
        columns = pl.ds(pl.multiple_of(part * WIDTH + z * 128, 128), 128)
        loads.append(
            pltpu.make_async_copy(
                w_in_ref.at[:, columns], w_raw.at[part], local_sem.at[part]
            )
        )
    loads.append(pltpu.make_async_copy(w_merge_ref, w_out, local_sem.at[3]))
    for load in loads:
        load.start()

    own_rows = pl.ds(pl.multiple_of(c * CHUNK, CHUNK), CHUNK)
    xall[0, 0, c] = layer_norm(clip_ref[own_rows, :]).astype(BF16)

    lane = lax.broadcasted_iota(jnp.int32, (1, 128), 1)
    first_head = lane < 64

    chosen = (
        lax.broadcasted_iota(jnp.int32, (16, table_ref.shape[0]), 1) == ordinal_ref[0]
    ).astype(BF16)
    affine = jnp.dot(chosen, table_ref[...], preferred_element_type=F32)[:8] + pair_ref[
        ...
    ].astype(F32)
    shift = affine[:, :WIDTH]
    scale_now = strength_ref[0]
    step_now = increment_ref[0]
    share = jnp.where(c == 0, scale_now, 1.0 - scale_now) * step_now
    gates[c] = affine[:, 2 * WIDTH :] * share
    incs[k] = jnp.full((8, 128), step_now, F32)
    scale_column = jnp.transpose(
        jnp.broadcast_to(1.0 + affine[:1, WIDTH : 2 * WIDTH], (128, WIDTH))
    )
    shift_high = shift.astype(BF16)
    shift_low = shift - shift_high.astype(F32)
    shift_parts = jnp.concatenate([shift_high.astype(F32), shift_low], axis=0).astype(BF16)
    for part in range(3):
        loads[part].wait()
        raw = w_raw[part]
        both = jnp.dot(shift_parts, raw, preferred_element_type=F32)
        bias[:, part * 128 : (part + 1) * 128] = both[:8] + both[8:]
        w_mod[:, part * 128 : (part + 1) * 128] = (raw.astype(F32) * scale_column).astype(BF16)
    for h in range(2):
        vt[h, 64:, :] = jnp.ones((16, FRAMES), BF16)
    q_scale = jnp.where(first_head, sharp_ref[2 * z], sharp_ref[2 * z + 1]) * (
        LOG2E / math.sqrt(64.0)
    )
    same_head = (
        (lax.broadcasted_iota(jnp.int32, (128, 128), 0) < 64)
        == (lax.broadcasted_iota(jnp.int32, (128, 128), 1) < 64)
    ).astype(F32).astype(BF16)

    pl.semaphore_wait(barrier, 2 * (COLUMN - 1))

    def left_all(block, send_sem):
        remote(block, block, send_sem, pair_recv.at[0], {"cfg": other}).wait_send()

    def came_all(block, recv_sem):
        remote(block, block, pair_send.at[0], recv_sem, {"cfg": other}).wait_recv()

    def rel(offset):
        return lax.rem(offset * sign + RING, RING)

    def half_rows(h):
        return pl.ds(h * HALF, HALF)

    def at(t, offset, core, h):
        return xall.at[t, rel(offset), core, half_rows(h)]

    z_major = lax.rem(z + sign + RING, RING)
    z_minor = lax.rem(z - sign + RING, RING)

    def major(t, i, h):
        return remote(
            at(t, -i, c, h),
            at(t, -(i + 1), c, h),
            maj_send.at[t],
            ring_recv.at[t, rel(-(i + 1)), c, h],
            {"seq": z_major},
        )

    def minor(t, i, h):
        return remote(
            at(t, i, c, h),
            at(t, i + 1, c, h),
            min_send.at[t],
            ring_recv.at[t, rel(i + 1), c, h],
            {"seq": z_minor},
        )

    def across(t, offset, h, core):
        block = at(t, offset, core, h)
        return remote(
            block,
            block,
            d2d_send.at[t],
            ring_recv.at[t, rel(offset), core, h],
            {"cfg": other},
        )

    def begin(t, h):
        major(t, 0, h).start()
        minor(t, 0, h).start()
        across(t, 0, h, c).start()

    def onward(t, i, h, hops):
        major(t, i - 1, h).wait_recv()
        if i < hops:
            major(t, i, h).start()
        across(t, -i, h, c).start()
        if i < 4:
            minor(t, i - 1, h).wait_recv()
            if i < min(hops, 3):
                minor(t, i, h).start()
            across(t, i, h, c).start()

    def other_half_came(t, offset):
        for h in range(2):
            across(t, offset, h, other).wait_recv()

    x, y = lax.rem(k, 4), k // 4
    one, two = x + c * (y - x), y + c * (x - y)
    step_one, step_two = 1 + 3 * c, 4 - 3 * c

    def piece_rows(index):
        return pl.ds(pl.multiple_of(index * 32, 32), 32)

    def piece_lanes(index):
        return pl.ds(pl.multiple_of(index * 256, 256), 256)

    def far_copy(i):
        return remote(
            xall.at[0, 0, c, piece_rows(two), piece_lanes(one)],
            xall.at[0, 3 + i, c, piece_rows(two), piece_lanes(one)],
            far_send.at[0],
            far_recv.at[0],
            {"seq": lax.rem(z + 5 - i, RING)},
        )

    def plane_one(o):
        peer = lax.rem(one + o, 4)
        block = xall.at[0, pl.ds(3, 3), c, piece_rows(two), piece_lanes(one)]
        return remote(
            block,
            block,
            plane_send.at[0],
            plane_recv.at[0],
            {"step": k + (peer - one) * step_one},
        )

    def plane_two(o):
        peer = lax.rem(two + o, 4)
        block = xall.at[0, pl.ds(3, 3), c, piece_rows(two)]
        return remote(
            block,
            block,
            plane_send.at[1],
            plane_recv.at[1],
            {"step": k + (peer - two) * step_two},
        )

    def plane_across(core):
        block = xall.at[0, pl.ds(3, 3), core]
        return remote(block, block, far_send.at[1], far_recv.at[1], {"cfg": other})

    far_bytes = xall.at[0, pl.ds(0, 3), 0, pl.ds(0, 32), pl.ds(0, 256)]
    one_bytes = xall.at[0, pl.ds(0, 3), 0, pl.ds(0, 32), pl.ds(0, 768)]
    two_bytes = xall.at[0, pl.ds(0, 3), 0, pl.ds(0, 96)]

    for i in range(3):
        far_copy(i).start()
    for h in range(2):
        begin(0, h)
    gate_copy = remote(
        gates.at[c], gates.at[c], pair_send.at[0], pair_recv.at[0], {"cfg": other}
    )
    gate_copy.start()

    def inc_copy(o):
        return remote(
            incs.at[k],
            incs.at[k],
            inc_send.at[0],
            inc_recv.at[0],
            {"step": lax.rem(k + o, STEPS)},
        )

    def send_inc(o, carry):
        inc_copy(o).start()
        return carry

    def project(t, start, slots):
        rows = len(slots) * CHUNK
        block = jnp.concatenate([xall[t, slab, core] for slab, core in slots], axis=0)
        qkv = jnp.dot(block, w_mod[...], preferred_element_type=F32) + bias[:1, :]
        here = pl.ds(start, rows)

        def normalize(values):
            squares = jnp.dot(
                (values * values).astype(BF16), same_head, preferred_element_type=F32
            )
            return values * lax.rsqrt(squares * (1.0 / 64.0) + 1e-06)

        queries = normalize(qkv[:, :128]) * q_scale
        for i in range(0, rows, TILE):
            parts = [queries[i + r : i + r + HALF] for r in (0, CHUNK, HALF, CHUNK + HALF)]
            qb[pl.ds(start + i, TILE), :] = jnp.concatenate(parts, axis=0).astype(BF16)
        keys = normalize(qkv[:, 128:256])
        values = jnp.transpose(qkv[:, 256:])
        for h in range(2):
            mask = first_head if h == 0 else jnp.logical_not(first_head)
            kb[h, here, :] = jnp.where(mask, keys, 0.0).astype(BF16)
            vt[h, :64, here] = values[h * 64 : (h + 1) * 64].astype(BF16)

    def attend(q, low, high, totals):
        totals = list(totals)
        for j in range(low, high, 1024):
            end = min(j + 1024, high)
            for h in range(2):
                scores = lax.dot_general(
                    kb[h, j:end, :], q, (((1,), (1,)), ((), ())), preferred_element_type=F32
                )
                powers = jnp.exp2(scores).astype(BF16)
                totals[h] = totals[h] + jnp.dot(
                    vt[h, :, j:end], powers, preferred_element_type=F32
                )
        return totals

    def zeros(count):
        return [jnp.zeros((80, count), F32)] * 2

    def pieces(low, high):
        count = -(-(high - low) // 1024)
        each = (high - low) // count
        return [(low + n * each, low + (n + 1) * each) for n in range(count)]

    def older(low, high):
        for a, b in pieces(0, low):
            totals = attend(qb[a:b, :], low, high, [acc[0, :, a:b], acc[1, :, a:b]])
            for h in range(2):
                acc[h, :, a:b] = totals[h]

    def newer(low, high, last):
        for a, b in pieces(low, high):
            totals = attend(qb[a:b, :], 0, last, zeros(b - a))
            for h in range(2):
                acc[h, :, a:b] = totals[h]

    def place(t, i):
        if t == 0 and i > 4:
            return i - 2
        return rel(-(i + 1) // 2 if i % 2 else i // 2)

    def result_copy(t, h, i, side):
        target = {"seq": lax.rem(z + place(t, i), RING), "cfg": c if side == 0 else other}
        return remote(
            ob.at[t, h, 2 * i + side],
            att.at[t, h, c, z],
            a2a_send.at[t, h],
            a2a_recv.at[t, h],
            target,
        )

    def both(slab):
        return [(slab, c), (slab, other)]

    def gather_first():
        other_half_came(0, 0)
        project(0, 0, both(0))
        newer(0, TILE, TILE)
        came_all(far_bytes, far_recv.at[0])
        for o in (2, 1, 3):
            plane_one(o).start()
        lax.fori_loop(1, STEPS, send_inc, 0)
        onward(0, 1, 0, 2)
        onward(0, 1, 1, 2)
        came_all(one_bytes, plane_recv.at[0])
        for o in (2, 1, 3):
            plane_two(o).start()
        other_half_came(0, -1)
        other_half_came(0, 1)
        project(0, 256, both(rel(-1)) + both(rel(1)))
        older(256, 768)
        newer(256, 768, 768)
        onward(0, 2, 0, 2)
        onward(0, 2, 1, 2)
        other_half_came(0, -2)
        other_half_came(0, 2)
        project(0, 768, both(rel(-2)) + both(rel(2)))
        older(768, 1280)
        came_all(two_bytes, plane_recv.at[1])
        plane_across(c).start()
        newer(768, 1280, 1280)
        plane_across(other).wait_recv()
        project(0, 1280, both(3) + both(4) + both(5))
        finish(0, 1280, (3, 4, 1, 2, 0), (6, 5, 7))

    def gather_second():
        other_half_came(1, 0)
        project(1, 0, both(0))
        newer(0, TILE, TILE)
        onward(1, 2, 0, 4)
        for i in range(1, 5):
            if i < 4:
                onward(1, i, 1, 4)
            other_half_came(1, -i)
            slots = both(rel(-i))
            if i < 4:
                other_half_came(1, i)
                slots = slots + both(rel(i))
            low = TILE + 2 * TILE * (i - 1)
            high = low + len(slots) * CHUNK
            project(1, low, slots)
            if i < 4:
                older(low, high)
                if i < 3:
                    onward(1, i + 2, 0, 4)
                else:
                    onward(1, 4, 1, 4)
                newer(low, high, high)
        finish(1, FRAMES - TILE, (5, 6, 3, 4, 1, 2, 0), (7,))

    def each_result(t, h, order, act):
        for i in order:
            for side in range(2):
                if i or side:
                    act(result_copy(t, h, i, side))

    def finish(t, last, old, new):
        def settle(half, order, low):
            starts = [i * TILE + half * CHUNK for i in order]
            totals = attend(
                jnp.concatenate([qb[r : r + CHUNK, :] for r in starts], axis=0),
                low,
                FRAMES,
                [
                    jnp.concatenate([acc[h, :, r : r + CHUNK] for r in starts], axis=1)
                    for h in range(2)
                ]
                if low
                else zeros(CHUNK * len(order)),
            )
            result = jnp.transpose(
                jnp.concatenate([a[:64] * (1.0 / a[64:65]) for a in totals], axis=0)
            ).astype(BF16)
            for n, i in enumerate(order):
                for side in range(2):
                    start = n * CHUNK + side * HALF
                    piece = result[start : start + HALF]
                    if i == 0 and side == 0:
                        att[t, half, c, z] = piece
                    else:
                        ob[t, half, 2 * i + side] = piece
            each_result(t, half, order, lambda copy: copy.start())

        settle(0, old, last)
        settle(0, new, 0)
        settle(1, old, last)
        settle(1, new, 0)

    colour = lax.rem(x + y, 2)

    def owner(spot, h):
        return 2 * spot + lax.rem(spot // 2 + h, 2)

    def clip_rows():
        start = c * CHUNK + colour * HALF + k // 2 * 8
        return clip_ref[pl.ds(pl.multiple_of(start, 8), 8), :]

    def term_copy(t, h, j):
        spot = lax.rem(j + k // 2, 8)
        return remote(
            sb.at[t, h, spot],
            rb.at[t, k],
            s_send.at[t],
            s_recv.at[t],
            {"step": owner(spot, h)},
        )

    def each_owner(t, h, act):
        def one_owner(j, carry):
            @pl.when(owner(lax.rem(j + k // 2, 8), h) != k)
            def _():
                act(term_copy(t, h, j))

            return carry

        lax.fori_loop(0, 8, one_owner, 0)

    def back_copy(t, o):
        target = lax.rem(k + o, STEPS)
        return remote(
            nb.at[t, target],
            nr.at[t, colour, k // 2],
            n_send.at[t],
            n_recv.at[t, colour],
            {"step": target},
        )

    def merge(t, h):
        came_all(ob.at[t, h, pl.ds(0, COLUMN - 1)], a2a_recv.at[t, h])
        attended = jnp.concatenate(
            [
                jnp.concatenate([att[t, h, cc, zz] for zz in range(RING)], axis=1)
                for cc in range(2)
            ],
            axis=0,
        )
        projected = jnp.dot(attended, w_out[...], preferred_element_type=F32)
        terms = projected[:HALF] * gates[0, :1, :] + projected[HALF:] * gates[1, :1, :]
        sb[t, h] = fold(terms.reshape(8, 8, WIDTH))

    def send_terms(t, h):
        each_owner(t, h, lambda copy: copy.start())

    def own(t, h):
        @pl.when(colour == h)
        def _():
            rb[t, k] = sb[t, h, k // 2]

            came_all(rb.at[t, pl.ds(0, STEPS - 1)], s_recv.at[t])
            terms = unfold(rb[t])
            start_rows = clip_rows()
            total = jnp.zeros_like(start_rows)
            if t == 0:
                for j in range(STEPS):
                    states[j] = start_rows + total
                    total = total + (increment(j) * start_rows + terms[j])
                nb[0] = fold(layer_norm(states[...]))
            else:
                drifts = []
                for j in range(STEPS):
                    total = total + (increment(j) * states[j] + terms[j])
                    drifts.append(total)
                nb[1] = fold(jnp.stack(drifts, axis=0))

            def back(o, carry):
                back_copy(t, o).start()
                return carry

            lax.fori_loop(1, STEPS, back, 0)
            nr[t, h, k // 2] = nb[t, k]

    def rows_back(t, h):
        @pl.when(colour == h)
        def _():
            came_all(nr.at[t, h, pl.ds(0, 7)], n_recv.at[t, h])

        @pl.when(colour != h)
        def _():
            came_all(nr.at[t, h], n_recv.at[t, h])

        return unfold(nr[t, h]).reshape(HALF, WIDTH)

    def next_rows(h):
        xall[1, 0, c, half_rows(h)] = rows_back(0, h).astype(BF16)
        begin(1, h)

    def final_copy(h):
        return remote(
            nr.at[1, h], fin.at[h], pair_send.at[1 + h], pair_recv.at[1 + h], {"cfg": other}
        )

    def out_copy(rows, i):
        return pltpu.make_async_copy(
            out_rows.at[rows], out_ref.at[rows], local_sem.at[4 + i]
        )

    def own_out(h):
        rows = pl.ds(pl.multiple_of(c * CHUNK + h * HALF, HALF), HALF)
        drift = rows_back(1, h)
        final_copy(h).start()
        out_rows[rows, :] = clip_ref[rows, :] + drift
        out_copy(rows, h).start()

    def increment(j):
        return jnp.concatenate([incs[j]] * (WIDTH // 128), axis=1)

    def results_left(t):
        for h in range(2):
            left_all(ob.at[t, h, pl.ds(0, COLUMN - 1)], a2a_send.at[t, h])

    def ring_left(t):
        hops = (2, 4)[t]
        left_all(xall.at[t, pl.ds(0, hops), 0], maj_send.at[t])
        left_all(xall.at[t, pl.ds(0, min(hops, 3)), 0], min_send.at[t])
        left_all(xall.at[t, pl.ds(0, 5 if hops == 2 else RING), 0], d2d_send.at[t])

    def exchange_left(t):
        left_all(nb.at[t, pl.ds(0, STEPS - 1)], n_send.at[t])
        left_all(rb.at[t, pl.ds(0, STEPS - 1)], s_send.at[t])

    gather_first()
    loads[3].wait()
    gate_copy_back = remote(
        gates.at[other], gates.at[other], pair_send.at[0], pair_recv.at[0], {"cfg": other}
    )
    gate_copy_back.wait_recv()

    came_all(incs.at[pl.ds(0, STEPS - 1)], inc_recv.at[0])
    merge(0, 0)
    send_terms(0, 0)
    own(0, 0)
    merge(0, 1)
    send_terms(0, 1)
    next_rows(0)
    own(0, 1)
    onward(1, 1, 0, 4)
    next_rows(1)

    gate_copy.wait_send()
    ring_left(0)
    exchange_left(0)
    results_left(0)
    left_all(incs.at[pl.ds(0, STEPS - 1)], inc_send.at[0])
    left_all(far_bytes, far_send.at[0])
    left_all(one_bytes, plane_send.at[0])
    left_all(two_bytes, plane_send.at[1])
    plane_across(c).wait_send()

    gather_second()
    ring_left(1)
    merge(1, 0)
    merge(1, 1)
    send_terms(1, 0)
    send_terms(1, 1)
    results_left(1)
    for h in range(2):
        own(1, h)
    own_out(0)
    own_out(1)
    for h in range(2):
        rows = pl.ds(pl.multiple_of(other * CHUNK + h * HALF, HALF), HALF)
        final_copy(h).wait_recv()
        out_rows[rows, :] = clip_ref[rows, :] + unfold(fin[h]).reshape(HALF, WIDTH)
        out_copy(rows, 2 + h).start()
    exchange_left(1)
    for h in range(2):
        final_copy(h).wait_send()
        out_copy(half_rows(h), h).wait()
        out_copy(half_rows(h), 2 + h).wait()


def local(clip, ordinal, strength, increment, table, pair, w_in, w_merge, sharp):
    vmem = pl.BlockSpec(memory_space=pltpu.VMEM)
    smem = pl.BlockSpec(memory_space=pltpu.SMEM)
    anywhere = pl.BlockSpec(memory_space=pl.ANY)
    dma = pltpu.SemaphoreType.DMA
    out = pl.pallas_call(
        kernel,
        out_shape=jax.ShapeDtypeStruct(clip.shape, F32),
        in_specs=[vmem, smem, smem, smem, vmem, vmem, anywhere, anywhere, smem],
        out_specs=anywhere,
        scratch_shapes=[
            pltpu.VMEM((2, RING, 2, CHUNK, WIDTH), BF16),
            pltpu.VMEM((3, WIDTH, 128), BF16),
            pltpu.VMEM((WIDTH, 384), BF16),
            pltpu.VMEM((WIDTH, WIDTH), BF16),
            pltpu.VMEM((8, 384), F32),
            pltpu.VMEM((FRAMES, 128), BF16),
            pltpu.VMEM((2, FRAMES, 128), BF16),
            pltpu.VMEM((2, 80, FRAMES), BF16),
            pltpu.VMEM((2, 80, FRAMES), F32),
            pltpu.VMEM((2, 2, COLUMN, HALF, 128), BF16),
            pltpu.VMEM((2, 2, 2, RING, HALF, 128), BF16),
            pltpu.VMEM((2, 2, 8, 16, 512), BF16),
            pltpu.VMEM((2, STEPS, 16, 512), BF16),
            pltpu.VMEM((2, STEPS, 16, 512), BF16),
            pltpu.VMEM((2, 2, 8, 16, 512), BF16),
            pltpu.VMEM((2, 8, 16, 512), BF16),
            pltpu.VMEM((STEPS, 8, WIDTH), F32),
            pltpu.VMEM((2, 8, WIDTH), F32),
            pltpu.VMEM((STEPS, 8, 128), F32),
            pltpu.VMEM((2 * CHUNK, WIDTH), F32),
            dma((8,)),
            dma((2,)),
            dma((2,)),
            dma((2,)),
            dma((2, RING, 2, 2)),
            dma((2,)),
            dma((2,)),
            dma((2,)),
            dma((2,)),
            dma((2, 2)),
            dma((2, 2)),
            dma((2,)),
            dma((2,)),
            dma((2,)),
            dma((2, 2)),
            dma((1,)),
            dma((1,)),
            dma((3,)),
            dma((3,)),
        ],
        compiler_params=pltpu.CompilerParams(
            collective_id=0, has_side_effects=True, vmem_limit_bytes=56 * 2**20
        ),
    )(clip, ordinal, strength, increment, table, pair, w_in, w_merge, sharp)
    return out[None]


def solution(mesh):
    placed = (P("seq", None), P("step"), P("step"), P("step"), P(), P("cfg", None), P(), P(), P())
    return jax.shard_map(
        local, mesh=mesh, in_specs=placed, out_specs=P("step", "seq", None), check_vma=False
    )
```

```python
import math

import jax
import jax.numpy as jnp
from jax import lax
from jax.experimental import pallas as pl
from jax.experimental.pallas import tpu as pltpu
from jax.sharding import PartitionSpec as P

MESH = pl.DeviceIdType.MESH
F32 = jnp.float32
BF16 = jnp.bfloat16
LOG2E = 1.4426950408889634

WIDTH = 1024
FRAMES = 2048
HALF = 64
CHUNK = 128
TILE = 256
RING = 8
STEPS = 16
COLUMN = 16


def remote(src, dst, send_sem, recv_sem, device):
    return pltpu.make_async_remote_copy(
        src_ref=src,
        dst_ref=dst,
        send_sem=send_sem,
        recv_sem=recv_sem,
        device_id=device,
        device_id_type=MESH,
    )


def fold(rows):
    half = WIDTH // 2
    return jnp.concatenate([rows[:, :, :half], rows[:, :, half:]], axis=1).astype(BF16)


def unfold(tiles):
    wide = tiles.astype(F32)
    return jnp.concatenate([wide[:, :8], wide[:, 8:]], axis=2)


def layer_norm(rows):
    average = jnp.mean(rows, axis=-1, keepdims=True)
    centred = rows - average
    variance = jnp.mean(centred * centred, axis=-1, keepdims=True)
    return centred * lax.rsqrt(variance + 1e-06)


def kernel(
    clip_ref,
    ordinal_ref,
    strength_ref,
    increment_ref,
    table_ref,
    pair_ref,
    w_in_ref,
    w_merge_ref,
    sharp_ref,
    out_ref,
    xall,
    w_raw,
    w_mod,
    w_out,
    bias,
    qb,
    kb,
    vt,
    acc,
    ob,
    att,
    sb,
    rb,
    nb,
    nr,
    fin,
    states,
    gates,
    incs,
    out_rows,
    local_sem,
    maj_send,
    min_send,
    d2d_send,
    ring_recv,
    far_send,
    far_recv,
    plane_send,
    plane_recv,
    a2a_send,
    a2a_recv,
    s_send,
    s_recv,
    n_send,
    n_recv,
    inc_send,
    inc_recv,
    pair_send,
    pair_recv,
):
    k = lax.axis_index("step")
    c = lax.axis_index("cfg")
    z = lax.axis_index("seq")
    other = 1 - c
    sign = 1 - 2 * c
    mine = 2 * z + c

    barrier = pltpu.get_barrier_semaphore()

    def greet(o, carry):
        e = lax.rem(mine + o, COLUMN)
        pl.semaphore_signal(
            barrier, inc=1, device_id={"seq": e // 2, "cfg": lax.rem(e, 2)}, device_id_type=MESH
        )
        pl.semaphore_signal(
            barrier, inc=1, device_id={"step": lax.rem(k + o, STEPS)}, device_id_type=MESH
        )
        return carry

    lax.fori_loop(1, COLUMN, greet, 0)

    loads = []
    for part in range(3):
        columns = pl.ds(pl.multiple_of(part * WIDTH + z * 128, 128), 128)
        loads.append(
            pltpu.make_async_copy(
                w_in_ref.at[:, columns], w_raw.at[part], local_sem.at[part]
            )
        )
    loads.append(pltpu.make_async_copy(w_merge_ref, w_out, local_sem.at[3]))
    for load in loads:
        load.start()

    own_rows = pl.ds(pl.multiple_of(c * CHUNK, CHUNK), CHUNK)
    xall[0, 0, c] = layer_norm(clip_ref[own_rows, :]).astype(BF16)

    lane = lax.broadcasted_iota(jnp.int32, (1, 128), 1)
    first_head = lane < 64

    chosen = (
        lax.broadcasted_iota(jnp.int32, (16, table_ref.shape[0]), 1) == ordinal_ref[0]
    ).astype(BF16)
    affine = jnp.dot(chosen, table_ref[...], preferred_element_type=F32)[:8] + pair_ref[
        ...
    ].astype(F32)
    shift = affine[:, :WIDTH]
    scale_now = strength_ref[0]
    step_now = increment_ref[0]
    share = jnp.where(c == 0, scale_now, 1.0 - scale_now) * step_now
    gates[c] = affine[:, 2 * WIDTH :] * share
    incs[k] = jnp.full((8, 128), step_now, F32)
    scale_column = jnp.transpose(
        jnp.broadcast_to(1.0 + affine[:1, WIDTH : 2 * WIDTH], (128, WIDTH))
    )
    shift_high = shift.astype(BF16)
    shift_low = shift - shift_high.astype(F32)
    shift_parts = jnp.concatenate([shift_high.astype(F32), shift_low], axis=0).astype(BF16)
    for part in range(3):
        loads[part].wait()
        raw = w_raw[part]
        both = jnp.dot(shift_parts, raw, preferred_element_type=F32)
        bias[:, part * 128 : (part + 1) * 128] = both[:8] + both[8:]
        w_mod[:, part * 128 : (part + 1) * 128] = (raw.astype(F32) * scale_column).astype(BF16)
    for h in range(2):
        vt[h, 64:, :] = jnp.ones((16, FRAMES), BF16)
    q_scale = jnp.where(first_head, sharp_ref[2 * z], sharp_ref[2 * z + 1]) * (
        LOG2E / math.sqrt(64.0)
    )
    same_head = (
        (lax.broadcasted_iota(jnp.int32, (128, 128), 0) < 64)
        == (lax.broadcasted_iota(jnp.int32, (128, 128), 1) < 64)
    ).astype(F32).astype(BF16)

    pl.semaphore_wait(barrier, 2 * (COLUMN - 1))

    def left_all(block, send_sem):
        remote(block, block, send_sem, pair_recv.at[0], {"cfg": other}).wait_send()

    def came_all(block, recv_sem):
        remote(block, block, pair_send.at[0], recv_sem, {"cfg": other}).wait_recv()

    def rel(offset):
        return lax.rem(offset * sign + RING, RING)

    def half_rows(h):
        return pl.ds(h * HALF, HALF)

    def at(t, offset, core, h):
        return xall.at[t, rel(offset), core, half_rows(h)]

    z_major = lax.rem(z + sign + RING, RING)
    z_minor = lax.rem(z - sign + RING, RING)

    def major(t, i, h):
        return remote(
            at(t, -i, c, h),
            at(t, -(i + 1), c, h),
            maj_send.at[t],
            ring_recv.at[t, rel(-(i + 1)), c, h],
            {"seq": z_major},
        )

    def minor(t, i, h):
        return remote(
            at(t, i, c, h),
            at(t, i + 1, c, h),
            min_send.at[t],
            ring_recv.at[t, rel(i + 1), c, h],
            {"seq": z_minor},
        )

    def across(t, offset, h, core):
        block = at(t, offset, core, h)
        return remote(
            block,
            block,
            d2d_send.at[t],
            ring_recv.at[t, rel(offset), core, h],
            {"cfg": other},
        )

    def begin(t, h):
        major(t, 0, h).start()
        minor(t, 0, h).start()
        across(t, 0, h, c).start()

    def onward(t, i, h, hops):
        major(t, i - 1, h).wait_recv()
        if i < hops:
            major(t, i, h).start()
        across(t, -i, h, c).start()
        if i < 4:
            minor(t, i - 1, h).wait_recv()
            if i < min(hops, 3):
                minor(t, i, h).start()
            across(t, i, h, c).start()

    def other_half_came(t, offset):
        for h in range(2):
            across(t, offset, h, other).wait_recv()

    x, y = lax.rem(k, 4), k // 4
    one, two = x + c * (y - x), y + c * (x - y)
    step_one, step_two = 1 + 3 * c, 4 - 3 * c

    def piece_rows(index):
        return pl.ds(pl.multiple_of(index * 32, 32), 32)

    def piece_lanes(index):
        return pl.ds(pl.multiple_of(index * 256, 256), 256)

    def far_copy(i):
        return remote(
            xall.at[0, 0, c, piece_rows(two), piece_lanes(one)],
            xall.at[0, 3 + i, c, piece_rows(two), piece_lanes(one)],
            far_send.at[0],
            far_recv.at[0],
            {"seq": lax.rem(z + 5 - i, RING)},
        )

    def plane_one(o):
        peer = lax.rem(one + o, 4)
        block = xall.at[0, pl.ds(3, 3), c, piece_rows(two), piece_lanes(one)]
        return remote(
            block,
            block,
            plane_send.at[0],
            plane_recv.at[0],
            {"step": k + (peer - one) * step_one},
        )

    def plane_two(o):
        peer = lax.rem(two + o, 4)
        block = xall.at[0, pl.ds(3, 3), c, piece_rows(two)]
        return remote(
            block,
            block,
            plane_send.at[1],
            plane_recv.at[1],
            {"step": k + (peer - two) * step_two},
        )

    def plane_across(core):
        block = xall.at[0, pl.ds(3, 3), core]
        return remote(block, block, far_send.at[1], far_recv.at[1], {"cfg": other})

    far_bytes = xall.at[0, pl.ds(0, 3), 0, pl.ds(0, 32), pl.ds(0, 256)]
    one_bytes = xall.at[0, pl.ds(0, 3), 0, pl.ds(0, 32), pl.ds(0, 768)]
    two_bytes = xall.at[0, pl.ds(0, 3), 0, pl.ds(0, 96)]

    for i in range(3):
        far_copy(i).start()
    for h in range(2):
        begin(0, h)
    gate_copy = remote(
        gates.at[c], gates.at[c], pair_send.at[0], pair_recv.at[0], {"cfg": other}
    )
    gate_copy.start()

    def inc_copy(o):
        return remote(
            incs.at[k],
            incs.at[k],
            inc_send.at[0],
            inc_recv.at[0],
            {"step": lax.rem(k + o, STEPS)},
        )

    def send_inc(o, carry):
        inc_copy(o).start()
        return carry

    def project(t, start, slots):
        rows = len(slots) * CHUNK
        block = jnp.concatenate([xall[t, slab, core] for slab, core in slots], axis=0)
        qkv = jnp.dot(block, w_mod[...], preferred_element_type=F32) + bias[:1, :]
        here = pl.ds(start, rows)

        def normalize(values):
            squares = jnp.dot(
                (values * values).astype(BF16), same_head, preferred_element_type=F32
            )
            return values * lax.rsqrt(squares * (1.0 / 64.0) + 1e-06)

        queries = normalize(qkv[:, :128]) * q_scale
        for i in range(0, rows, TILE):
            parts = [queries[i + r : i + r + HALF] for r in (0, CHUNK, HALF, CHUNK + HALF)]
            qb[pl.ds(start + i, TILE), :] = jnp.concatenate(parts, axis=0).astype(BF16)
        keys = normalize(qkv[:, 128:256])
        values = jnp.transpose(qkv[:, 256:])
        for h in range(2):
            mask = first_head if h == 0 else jnp.logical_not(first_head)
            kb[h, here, :] = jnp.where(mask, keys, 0.0).astype(BF16)
            vt[h, :64, here] = values[h * 64 : (h + 1) * 64].astype(BF16)

    def attend(q, low, high, totals):
        totals = list(totals)
        for j in range(low, high, 1024):
            end = min(j + 1024, high)
            for h in range(2):
                scores = lax.dot_general(
                    kb[h, j:end, :], q, (((1,), (1,)), ((), ())), preferred_element_type=F32
                )
                powers = jnp.exp2(scores).astype(BF16)
                totals[h] = totals[h] + jnp.dot(
                    vt[h, :, j:end], powers, preferred_element_type=F32
                )
        return totals

    def zeros(count):
        return [jnp.zeros((80, count), F32)] * 2

    def pieces(low, high):
        count = -(-(high - low) // 1024)
        each = (high - low) // count
        return [(low + n * each, low + (n + 1) * each) for n in range(count)]

    def older(low, high):
        for a, b in pieces(0, low):
            totals = attend(qb[a:b, :], low, high, [acc[0, :, a:b], acc[1, :, a:b]])
            for h in range(2):
                acc[h, :, a:b] = totals[h]

    def newer(low, high, last):
        for a, b in pieces(low, high):
            totals = attend(qb[a:b, :], 0, last, zeros(b - a))
            for h in range(2):
                acc[h, :, a:b] = totals[h]

    def place(t, i):
        if t == 0 and i > 4:
            return i - 2
        return rel(-(i + 1) // 2 if i % 2 else i // 2)

    def result_copy(t, h, i, side):
        target = {"seq": lax.rem(z + place(t, i), RING), "cfg": c if side == 0 else other}
        return remote(
            ob.at[t, h, 2 * i + side],
            att.at[t, h, c, z],
            a2a_send.at[t, h],
            a2a_recv.at[t, h],
            target,
        )

    def both(slab):
        return [(slab, c), (slab, other)]

    def gather_first():
        other_half_came(0, 0)
        project(0, 0, both(0))
        newer(0, TILE, TILE)
        came_all(far_bytes, far_recv.at[0])
        for o in (2, 1, 3):
            plane_one(o).start()
        lax.fori_loop(1, STEPS, send_inc, 0)
        onward(0, 1, 0, 2)
        onward(0, 1, 1, 2)
        came_all(one_bytes, plane_recv.at[0])
        for o in (2, 1, 3):
            plane_two(o).start()
        other_half_came(0, -1)
        other_half_came(0, 1)
        project(0, 256, both(rel(-1)) + both(rel(1)))
        older(256, 768)
        newer(256, 768, 768)
        onward(0, 2, 0, 2)
        onward(0, 2, 1, 2)
        other_half_came(0, -2)
        other_half_came(0, 2)
        project(0, 768, both(rel(-2)) + both(rel(2)))
        older(768, 1280)
        came_all(two_bytes, plane_recv.at[1])
        plane_across(c).start()
        newer(768, 1280, 1280)
        plane_across(other).wait_recv()
        project(0, 1280, both(3) + both(4) + both(5))
        finish(0, 1280, (3, 4, 1, 2, 0), (6, 5, 7))

    def gather_second():
        other_half_came(1, 0)
        project(1, 0, both(0))
        newer(0, TILE, TILE)
        onward(1, 1, 1, 4)
        for i in range(1, 5):
            other_half_came(1, -i)
            slots = both(rel(-i))
            if i < 4:
                other_half_came(1, i)
                slots = slots + both(rel(i))
            low = TILE + 2 * TILE * (i - 1)
            high = low + len(slots) * CHUNK
            project(1, low, slots)
            if i < 4:
                older(low, high)
                onward(1, i + 1, 0, 4)
                newer(low, high, high)
                onward(1, i + 1, 1, 4)
        finish(1, FRAMES - TILE, (5, 6, 3, 4, 1, 2, 0), (7,))

    def each_result(t, h, order, act):
        for i in order:
            for side in range(2):
                if i or side:
                    act(result_copy(t, h, i, side))

    def finish(t, last, old, new):
        def settle(half, order, low):
            starts = [i * TILE + half * CHUNK for i in order]
            totals = attend(
                jnp.concatenate([qb[r : r + CHUNK, :] for r in starts], axis=0),
                low,
                FRAMES,
                [
                    jnp.concatenate([acc[h, :, r : r + CHUNK] for r in starts], axis=1)
                    for h in range(2)
                ]
                if low
                else zeros(CHUNK * len(order)),
            )
            result = jnp.transpose(
                jnp.concatenate([a[:64] * (1.0 / a[64:65]) for a in totals], axis=0)
            ).astype(BF16)
            for n, i in enumerate(order):
                for side in range(2):
                    start = n * CHUNK + side * HALF
                    piece = result[start : start + HALF]
                    if i == 0 and side == 0:
                        att[t, half, c, z] = piece
                    else:
                        ob[t, half, 2 * i + side] = piece
            each_result(t, half, order, lambda copy: copy.start())

        settle(0, old, last)
        settle(0, new, 0)
        settle(1, old, last)
        settle(1, new, 0)

    colour = lax.rem(x + y, 2)

    def owner(spot, h):
        return 2 * spot + lax.rem(spot // 2 + h, 2)

    def clip_rows():
        start = c * CHUNK + colour * HALF + k // 2 * 8
        return clip_ref[pl.ds(pl.multiple_of(start, 8), 8), :]

    def term_copy(t, h, j):
        spot = lax.rem(j + k // 2, 8)
        return remote(
            sb.at[t, h, spot],
            rb.at[t, k],
            s_send.at[t],
            s_recv.at[t],
            {"step": owner(spot, h)},
        )

    def each_owner(t, h, act):
        def one_owner(j, carry):
            @pl.when(owner(lax.rem(j + k // 2, 8), h) != k)
            def _():
                act(term_copy(t, h, j))

            return carry

        lax.fori_loop(0, 8, one_owner, 0)

    def back_copy(t, o):
        target = lax.rem(k + o, STEPS)
        return remote(
            nb.at[t, target],
            nr.at[t, colour, k // 2],
            n_send.at[t],
            n_recv.at[t, colour],
            {"step": target},
        )

    def merge(t, h):
        came_all(ob.at[t, h, pl.ds(0, COLUMN - 1)], a2a_recv.at[t, h])
        attended = jnp.concatenate(
            [
                jnp.concatenate([att[t, h, cc, zz] for zz in range(RING)], axis=1)
                for cc in range(2)
            ],
            axis=0,
        )
        projected = jnp.dot(attended, w_out[...], preferred_element_type=F32)
        terms = projected[:HALF] * gates[0, :1, :] + projected[HALF:] * gates[1, :1, :]
        sb[t, h] = fold(terms.reshape(8, 8, WIDTH))

    def send_terms(t, h):
        each_owner(t, h, lambda copy: copy.start())

    def own(t, h):
        @pl.when(colour == h)
        def _():
            rb[t, k] = sb[t, h, k // 2]

            came_all(rb.at[t, pl.ds(0, STEPS - 1)], s_recv.at[t])
            terms = unfold(rb[t])
            start_rows = clip_rows()
            total = jnp.zeros_like(start_rows)
            if t == 0:
                for j in range(STEPS):
                    states[j] = start_rows + total
                    total = total + (increment(j) * start_rows + terms[j])
                nb[0] = fold(layer_norm(states[...]))
            else:
                drifts = []
                for j in range(STEPS):
                    total = total + (increment(j) * states[j] + terms[j])
                    drifts.append(total)
                nb[1] = fold(jnp.stack(drifts, axis=0))

            def back(o, carry):
                back_copy(t, o).start()
                return carry

            lax.fori_loop(1, STEPS, back, 0)
            nr[t, h, k // 2] = nb[t, k]

    def rows_back(t, h):
        @pl.when(colour == h)
        def _():
            came_all(nr.at[t, h, pl.ds(0, 7)], n_recv.at[t, h])

        @pl.when(colour != h)
        def _():
            came_all(nr.at[t, h], n_recv.at[t, h])

        return unfold(nr[t, h]).reshape(HALF, WIDTH)

    def next_rows(h):
        xall[1, 0, c, half_rows(h)] = rows_back(0, h).astype(BF16)
        begin(1, h)

    def final_copy(h):
        return remote(
            nr.at[1, h], fin.at[h], pair_send.at[1 + h], pair_recv.at[1 + h], {"cfg": other}
        )

    def out_copy(rows, i):
        return pltpu.make_async_copy(
            out_rows.at[rows], out_ref.at[rows], local_sem.at[4 + i]
        )

    def own_out(h):
        rows = pl.ds(pl.multiple_of(c * CHUNK + h * HALF, HALF), HALF)
        drift = rows_back(1, h)
        final_copy(h).start()
        out_rows[rows, :] = drift.astype(BF16)
        out_copy(rows, h).start()

    def increment(j):
        return jnp.concatenate([incs[j]] * (WIDTH // 128), axis=1)

    def results_left(t):
        for h in range(2):
            left_all(ob.at[t, h, pl.ds(0, COLUMN - 1)], a2a_send.at[t, h])

    def ring_left(t):
        hops = (2, 4)[t]
        left_all(xall.at[t, pl.ds(0, hops), 0], maj_send.at[t])
        left_all(xall.at[t, pl.ds(0, min(hops, 3)), 0], min_send.at[t])
        left_all(xall.at[t, pl.ds(0, 5 if hops == 2 else RING), 0], d2d_send.at[t])

    def exchange_left(t):
        left_all(nb.at[t, pl.ds(0, STEPS - 1)], n_send.at[t])
        left_all(rb.at[t, pl.ds(0, STEPS - 1)], s_send.at[t])

    gather_first()
    loads[3].wait()
    gate_copy_back = remote(
        gates.at[other], gates.at[other], pair_send.at[0], pair_recv.at[0], {"cfg": other}
    )
    gate_copy_back.wait_recv()

    came_all(incs.at[pl.ds(0, STEPS - 1)], inc_recv.at[0])
    for h in range(2):
        merge(0, h)
        send_terms(0, h)
    for h in range(2):
        own(0, h)
    next_rows(0)
    next_rows(1)
    onward(1, 1, 0, 4)

    gate_copy.wait_send()
    ring_left(0)
    exchange_left(0)
    results_left(0)
    left_all(incs.at[pl.ds(0, STEPS - 1)], inc_send.at[0])
    left_all(far_bytes, far_send.at[0])
    left_all(one_bytes, plane_send.at[0])
    left_all(two_bytes, plane_send.at[1])
    plane_across(c).wait_send()

    gather_second()
    ring_left(1)
    for h in range(2):
        merge(1, h)
        send_terms(1, h)
    results_left(1)
    for h in range(2):
        own(1, h)
    own_out(0)
    own_out(1)
    for h in range(2):
        rows = pl.ds(pl.multiple_of(other * CHUNK + h * HALF, HALF), HALF)
        final_copy(h).wait_recv()
        out_rows[rows, :] = unfold(fin[h]).reshape(HALF, WIDTH).astype(BF16)
        out_copy(rows, 2 + h).start()
    exchange_left(1)
    for h in range(2):
        final_copy(h).wait_send()
        out_copy(half_rows(h), h).wait()
        out_copy(half_rows(h), 2 + h).wait()


def local(clip, ordinal, strength, increment, table, pair, w_in, w_merge, sharp):
    vmem = pl.BlockSpec(memory_space=pltpu.VMEM)
    smem = pl.BlockSpec(memory_space=pltpu.SMEM)
    anywhere = pl.BlockSpec(memory_space=pl.ANY)
    dma = pltpu.SemaphoreType.DMA
    out = pl.pallas_call(
        kernel,
        out_shape=jax.ShapeDtypeStruct(clip.shape, BF16),
        in_specs=[vmem, smem, smem, smem, vmem, vmem, anywhere, anywhere, smem],
        out_specs=anywhere,
        scratch_shapes=[
            pltpu.VMEM((2, RING, 2, CHUNK, WIDTH), BF16),
            pltpu.VMEM((3, WIDTH, 128), BF16),
            pltpu.VMEM((WIDTH, 384), BF16),
            pltpu.VMEM((WIDTH, WIDTH), BF16),
            pltpu.VMEM((8, 384), F32),
            pltpu.VMEM((FRAMES, 128), BF16),
            pltpu.VMEM((2, FRAMES, 128), BF16),
            pltpu.VMEM((2, 80, FRAMES), BF16),
            pltpu.VMEM((2, 80, FRAMES), F32),
            pltpu.VMEM((2, 2, COLUMN, HALF, 128), BF16),
            pltpu.VMEM((2, 2, 2, RING, HALF, 128), BF16),
            pltpu.VMEM((2, 2, 8, 16, 512), BF16),
            pltpu.VMEM((2, STEPS, 16, 512), BF16),
            pltpu.VMEM((2, STEPS, 16, 512), BF16),
            pltpu.VMEM((2, 2, 8, 16, 512), BF16),
            pltpu.VMEM((2, 8, 16, 512), BF16),
            pltpu.VMEM((STEPS, 8, WIDTH), F32),
            pltpu.VMEM((2, 8, WIDTH), F32),
            pltpu.VMEM((STEPS, 8, 128), F32),
            pltpu.VMEM((2 * CHUNK, WIDTH), BF16),
            dma((8,)),
            dma((2,)),
            dma((2,)),
            dma((2,)),
            dma((2, RING, 2, 2)),
            dma((2,)),
            dma((2,)),
            dma((2,)),
            dma((2,)),
            dma((2, 2)),
            dma((2, 2)),
            dma((2,)),
            dma((2,)),
            dma((2,)),
            dma((2, 2)),
            dma((1,)),
            dma((1,)),
            dma((3,)),
            dma((3,)),
        ],
        compiler_params=pltpu.CompilerParams(
            collective_id=0, has_side_effects=True, vmem_limit_bytes=56 * 2**20
        ),
    )(clip, ordinal, strength, increment, table, pair, w_in, w_merge, sharp)
    return (clip + out.astype(F32))[None]


def solution(mesh):
    placed = (P("seq", None), P("step"), P("step"), P("step"), P(), P("cfg", None), P(), P(), P())
    return jax.shard_map(
        local, mesh=mesh, in_specs=placed, out_specs=P("step", "seq", None), check_vma=False
    )
```

```python
import math

import jax
import jax.numpy as jnp
from jax import lax
from jax.experimental import pallas as pl
from jax.experimental.pallas import tpu as pltpu
from jax.sharding import PartitionSpec as P

MESH = pl.DeviceIdType.MESH
F32 = jnp.float32
BF16 = jnp.bfloat16
LOG2E = 1.4426950408889634

WIDTH = 1024
FRAMES = 2048
HALF = 64
CHUNK = 128
TILE = 256
RING = 8
STEPS = 16
COLUMN = 16


def remote(src, dst, send_sem, recv_sem, device):
    return pltpu.make_async_remote_copy(
        src_ref=src,
        dst_ref=dst,
        send_sem=send_sem,
        recv_sem=recv_sem,
        device_id=device,
        device_id_type=MESH,
    )


def fold(rows):
    half = WIDTH // 2
    return jnp.concatenate([rows[:, :, :half], rows[:, :, half:]], axis=1).astype(BF16)


def unfold(tiles):
    wide = tiles.astype(F32)
    return jnp.concatenate([wide[:, :8], wide[:, 8:]], axis=2)


def layer_norm(rows):
    average = jnp.mean(rows, axis=-1, keepdims=True)
    centred = rows - average
    variance = jnp.mean(centred * centred, axis=-1, keepdims=True)
    return centred * lax.rsqrt(variance + 1e-06)


def kernel(
    clip_ref,
    ordinal_ref,
    strength_ref,
    increment_ref,
    table_ref,
    pair_ref,
    w_in_ref,
    w_merge_ref,
    sharp_ref,
    out_ref,
    xall,
    w_raw,
    w_mod,
    w_out,
    bias,
    qb,
    kb,
    vt,
    acc,
    ob,
    att,
    sb,
    rb,
    nb,
    nr,
    fin,
    states,
    gates,
    incs,
    out_rows,
    local_sem,
    maj_send,
    min_send,
    d2d_send,
    ring_recv,
    far_send,
    far_recv,
    plane_send,
    plane_recv,
    a2a_send,
    a2a_recv,
    s_send,
    s_recv,
    n_send,
    n_recv,
    inc_send,
    inc_recv,
    pair_send,
    pair_recv,
):
    k = lax.axis_index("step")
    c = lax.axis_index("cfg")
    z = lax.axis_index("seq")
    other = 1 - c
    sign = 1 - 2 * c
    mine = 2 * z + c

    barrier = pltpu.get_barrier_semaphore()

    def greet(o, carry):
        e = lax.rem(mine + o, COLUMN)
        pl.semaphore_signal(
            barrier, inc=1, device_id={"seq": e // 2, "cfg": lax.rem(e, 2)}, device_id_type=MESH
        )
        pl.semaphore_signal(
            barrier, inc=1, device_id={"step": lax.rem(k + o, STEPS)}, device_id_type=MESH
        )
        return carry

    lax.fori_loop(1, COLUMN, greet, 0)

    loads = []
    for part in range(3):
        columns = pl.ds(pl.multiple_of(part * WIDTH + z * 128, 128), 128)
        loads.append(
            pltpu.make_async_copy(
                w_in_ref.at[:, columns], w_raw.at[part], local_sem.at[part]
            )
        )
    loads.append(pltpu.make_async_copy(w_merge_ref, w_out, local_sem.at[3]))
    for load in loads:
        load.start()

    for core in range(2):
        rows = clip_ref[core * CHUNK : (core + 1) * CHUNK, :]
        xall[0, 0, core] = layer_norm(rows).astype(BF16)

    lane = lax.broadcasted_iota(jnp.int32, (1, 128), 1)
    first_head = lane < 64

    chosen = (
        lax.broadcasted_iota(jnp.int32, (16, table_ref.shape[0]), 1) == ordinal_ref[0]
    ).astype(BF16)
    affine = jnp.dot(chosen, table_ref[...], preferred_element_type=F32)[:8] + pair_ref[
        ...
    ].astype(F32)
    shift = affine[:, :WIDTH]
    scale_now = strength_ref[0]
    step_now = increment_ref[0]
    share = jnp.where(c == 0, scale_now, 1.0 - scale_now) * step_now
    gates[c] = affine[:, 2 * WIDTH :] * share
    incs[k] = jnp.full((8, 128), step_now, F32)
    scale_column = jnp.transpose(
        jnp.broadcast_to(1.0 + affine[:1, WIDTH : 2 * WIDTH], (128, WIDTH))
    )
    shift_high = shift.astype(BF16)
    shift_low = shift - shift_high.astype(F32)
    shift_parts = jnp.concatenate([shift_high.astype(F32), shift_low], axis=0).astype(BF16)
    for part in range(3):
        loads[part].wait()
        raw = w_raw[part]
        both = jnp.dot(shift_parts, raw, preferred_element_type=F32)
        bias[:, part * 128 : (part + 1) * 128] = both[:8] + both[8:]
        w_mod[:, part * 128 : (part + 1) * 128] = (raw.astype(F32) * scale_column).astype(BF16)
    for h in range(2):
        vt[h, 64:, :] = jnp.ones((16, FRAMES), BF16)
    q_scale = jnp.where(first_head, sharp_ref[2 * z], sharp_ref[2 * z + 1]) * (
        LOG2E / math.sqrt(64.0)
    )
    same_head = (
        (lax.broadcasted_iota(jnp.int32, (128, 128), 0) < 64)
        == (lax.broadcasted_iota(jnp.int32, (128, 128), 1) < 64)
    ).astype(F32).astype(BF16)

    def left_all(block, send_sem):
        remote(block, block, send_sem, pair_recv.at[0], {"cfg": other}).wait_send()

    def came_all(block, recv_sem):
        remote(block, block, pair_send.at[0], recv_sem, {"cfg": other}).wait_recv()

    def rel(offset):
        return lax.rem(offset * sign + RING, RING)

    def half_rows(h):
        return pl.ds(h * HALF, HALF)

    def at(t, offset, core, h):
        return xall.at[t, rel(offset), core, half_rows(h)]

    z_major = lax.rem(z + sign + RING, RING)
    z_minor = lax.rem(z - sign + RING, RING)

    def major(t, i, h):
        return remote(
            at(t, -i, c, h),
            at(t, -(i + 1), c, h),
            maj_send.at[t],
            ring_recv.at[t, rel(-(i + 1)), c, h],
            {"seq": z_major},
        )

    def minor(t, i, h):
        return remote(
            at(t, i, c, h),
            at(t, i + 1, c, h),
            min_send.at[t],
            ring_recv.at[t, rel(i + 1), c, h],
            {"seq": z_minor},
        )

    def across(t, offset, h, core):
        block = at(t, offset, core, h)
        return remote(
            block,
            block,
            d2d_send.at[t],
            ring_recv.at[t, rel(offset), core, h],
            {"cfg": other},
        )

    def begin(t, h):
        major(t, 0, h).start()
        minor(t, 0, h).start()
        if t:
            across(t, 0, h, c).start()

    def onward(t, i, h, hops):
        major(t, i - 1, h).wait_recv()
        if i < hops:
            major(t, i, h).start()
        across(t, -i, h, c).start()
        if i < 4:
            minor(t, i - 1, h).wait_recv()
            if i < min(hops, 3):
                minor(t, i, h).start()
            across(t, i, h, c).start()

    def other_half_came(t, offset):
        for h in range(2):
            across(t, offset, h, other).wait_recv()

    x, y = lax.rem(k, 4), k // 4
    one, two = x + c * (y - x), y + c * (x - y)
    step_one, step_two = 1 + 3 * c, 4 - 3 * c

    def piece_rows(index):
        return pl.ds(pl.multiple_of(index * 32, 32), 32)

    def piece_lanes(index):
        return pl.ds(pl.multiple_of(index * 256, 256), 256)

    def far_copy(i):
        return remote(
            xall.at[0, 0, c, piece_rows(two), piece_lanes(one)],
            xall.at[0, 3 + i, c, piece_rows(two), piece_lanes(one)],
            far_send.at[0],
            far_recv.at[0],
            {"seq": lax.rem(z + 5 - i, RING)},
        )

    def plane_one(o):
        peer = lax.rem(one + o, 4)
        block = xall.at[0, pl.ds(3, 3), c, piece_rows(two), piece_lanes(one)]
        return remote(
            block,
            block,
            plane_send.at[0],
            plane_recv.at[0],
            {"step": k + (peer - one) * step_one},
        )

    def plane_two(o):
        peer = lax.rem(two + o, 4)
        block = xall.at[0, pl.ds(3, 3), c, piece_rows(two)]
        return remote(
            block,
            block,
            plane_send.at[1],
            plane_recv.at[1],
            {"step": k + (peer - two) * step_two},
        )

    def plane_across(core):
        block = xall.at[0, pl.ds(3, 3), core]
        return remote(block, block, far_send.at[1], far_recv.at[1], {"cfg": other})

    far_bytes = xall.at[0, pl.ds(0, 3), 0, pl.ds(0, 32), pl.ds(0, 256)]
    one_bytes = xall.at[0, pl.ds(0, 3), 0, pl.ds(0, 32), pl.ds(0, 768)]
    two_bytes = xall.at[0, pl.ds(0, 3), 0, pl.ds(0, 96)]

    gate_copy = remote(
        gates.at[c], gates.at[c], pair_send.at[0], pair_recv.at[0], {"cfg": other}
    )

    def inc_copy(o):
        return remote(
            incs.at[k],
            incs.at[k],
            inc_send.at[0],
            inc_recv.at[0],
            {"step": lax.rem(k + o, STEPS)},
        )

    def send_inc(o, carry):
        inc_copy(o).start()
        return carry

    def project(t, start, slots):
        rows = len(slots) * CHUNK
        block = jnp.concatenate([xall[t, slab, core] for slab, core in slots], axis=0)
        qkv = jnp.dot(block, w_mod[...], preferred_element_type=F32) + bias[:1, :]
        here = pl.ds(start, rows)

        def normalize(values):
            squares = jnp.dot(
                (values * values).astype(BF16), same_head, preferred_element_type=F32
            )
            return values * lax.rsqrt(squares * (1.0 / 64.0) + 1e-06)

        queries = normalize(qkv[:, :128]) * q_scale
        for i in range(0, rows, TILE):
            parts = [queries[i + r : i + r + HALF] for r in (0, CHUNK, HALF, CHUNK + HALF)]
            qb[pl.ds(start + i, TILE), :] = jnp.concatenate(parts, axis=0).astype(BF16)
        keys = normalize(qkv[:, 128:256])
        values = jnp.transpose(qkv[:, 256:])
        for h in range(2):
            mask = first_head if h == 0 else jnp.logical_not(first_head)
            kb[h, here, :] = jnp.where(mask, keys, 0.0).astype(BF16)
            vt[h, :64, here] = values[h * 64 : (h + 1) * 64].astype(BF16)

    def attend(q, low, high, totals):
        totals = list(totals)
        for j in range(low, high, 1024):
            end = min(j + 1024, high)
            for h in range(2):
                scores = lax.dot_general(
                    kb[h, j:end, :], q, (((1,), (1,)), ((), ())), preferred_element_type=F32
                )
                powers = jnp.exp2(scores).astype(BF16)
                totals[h] = totals[h] + jnp.dot(
                    vt[h, :, j:end], powers, preferred_element_type=F32
                )
        return totals

    def zeros(count):
        return [jnp.zeros((80, count), F32)] * 2

    def pieces(low, high):
        count = -(-(high - low) // 1024)
        each = (high - low) // count
        return [(low + n * each, low + (n + 1) * each) for n in range(count)]

    def older(low, high):
        for a, b in pieces(0, low):
            totals = attend(qb[a:b, :], low, high, [acc[0, :, a:b], acc[1, :, a:b]])
            for h in range(2):
                acc[h, :, a:b] = totals[h]

    def newer(low, high, last):
        for a, b in pieces(low, high):
            totals = attend(qb[a:b, :], 0, last, zeros(b - a))
            for h in range(2):
                acc[h, :, a:b] = totals[h]

    project(0, 0, [(0, c), (0, other)])
    newer(0, TILE, TILE)
    pl.semaphore_wait(barrier, 2 * (COLUMN - 1))
    for i in range(3):
        far_copy(i).start()
    for h in range(2):
        begin(0, h)
    gate_copy.start()

    def place(t, i):
        if t == 0 and i > 4:
            return i - 2
        return rel(-(i + 1) // 2 if i % 2 else i // 2)

    def result_copy(t, h, i, side):
        target = {"seq": lax.rem(z + place(t, i), RING), "cfg": c if side == 0 else other}
        return remote(
            ob.at[t, h, 2 * i + side],
            att.at[t, h, c, z],
            a2a_send.at[t, h],
            a2a_recv.at[t, h],
            target,
        )

    def both(slab):
        return [(slab, c), (slab, other)]

    def gather_first():
        came_all(far_bytes, far_recv.at[0])
        for o in (2, 1, 3):
            plane_one(o).start()
        lax.fori_loop(1, STEPS, send_inc, 0)
        onward(0, 1, 0, 2)
        onward(0, 1, 1, 2)
        came_all(one_bytes, plane_recv.at[0])
        for o in (2, 1, 3):
            plane_two(o).start()
        other_half_came(0, -1)
        other_half_came(0, 1)
        project(0, 256, both(rel(-1)) + both(rel(1)))
        older(256, 768)
        newer(256, 768, 768)
        onward(0, 2, 0, 2)
        onward(0, 2, 1, 2)
        other_half_came(0, -2)
        other_half_came(0, 2)
        project(0, 768, both(rel(-2)) + both(rel(2)))
        older(768, 1280)
        came_all(two_bytes, plane_recv.at[1])
        plane_across(c).start()
        newer(768, 1280, 1280)
        plane_across(other).wait_recv()
        project(0, 1280, both(3) + both(4) + both(5))
        finish(0, 1280, (3, 4, 1, 2, 0), (6, 5, 7))

    def gather_second():
        other_half_came(1, 0)
        project(1, 0, both(0))
        newer(0, TILE, TILE)
        onward(1, 1, 1, 4)
        for i in range(1, 5):
            other_half_came(1, -i)
            slots = both(rel(-i))
            if i < 4:
                other_half_came(1, i)
                slots = slots + both(rel(i))
            low = TILE + 2 * TILE * (i - 1)
            high = low + len(slots) * CHUNK
            project(1, low, slots)
            if i < 4:
                older(low, high)
                onward(1, i + 1, 0, 4)
                newer(low, high, high)
                onward(1, i + 1, 1, 4)
        finish(1, FRAMES - TILE, (5, 6, 3, 4, 1, 2, 0), (7,))

    def each_result(t, h, order, act):
        for i in order:
            for side in range(2):
                if i or side:
                    act(result_copy(t, h, i, side))

    def finish(t, last, old, new):
        def settle(half, order, low):
            starts = [i * TILE + half * CHUNK for i in order]
            totals = attend(
                jnp.concatenate([qb[r : r + CHUNK, :] for r in starts], axis=0),
                low,
                FRAMES,
                [
                    jnp.concatenate([acc[h, :, r : r + CHUNK] for r in starts], axis=1)
                    for h in range(2)
                ]
                if low
                else zeros(CHUNK * len(order)),
            )
            result = jnp.transpose(
                jnp.concatenate([a[:64] * (1.0 / a[64:65]) for a in totals], axis=0)
            ).astype(BF16)
            for n, i in enumerate(order):
                for side in range(2):
                    start = n * CHUNK + side * HALF
                    piece = result[start : start + HALF]
                    if i == 0 and side == 0:
                        att[t, half, c, z] = piece
                    else:
                        ob[t, half, 2 * i + side] = piece
            each_result(t, half, order, lambda copy: copy.start())

        settle(0, old, last)
        settle(0, new, 0)
        settle(1, old, last)
        settle(1, new, 0)

    colour = lax.rem(x + y, 2)

    def owner(spot, h):
        return 2 * spot + lax.rem(spot // 2 + h, 2)

    def clip_rows():
        start = c * CHUNK + colour * HALF + k // 2 * 8
        return clip_ref[pl.ds(pl.multiple_of(start, 8), 8), :]

    def term_copy(t, h, j):
        spot = lax.rem(j + k // 2, 8)
        return remote(
            sb.at[t, h, spot],
            rb.at[t, k],
            s_send.at[t],
            s_recv.at[t],
            {"step": owner(spot, h)},
        )

    def each_owner(t, h, act):
        def one_owner(j, carry):
            @pl.when(owner(lax.rem(j + k // 2, 8), h) != k)
            def _():
                act(term_copy(t, h, j))

            return carry

        lax.fori_loop(0, 8, one_owner, 0)

    def back_copy(t, o):
        target = lax.rem(k + o, STEPS)
        return remote(
            nb.at[t, target],
            nr.at[t, colour, k // 2],
            n_send.at[t],
            n_recv.at[t, colour],
            {"step": target},
        )

    def merge(t, h):
        came_all(ob.at[t, h, pl.ds(0, COLUMN - 1)], a2a_recv.at[t, h])
        attended = jnp.concatenate(
            [
                jnp.concatenate([att[t, h, cc, zz] for zz in range(RING)], axis=1)
                for cc in range(2)
            ],
            axis=0,
        )
        projected = jnp.dot(attended, w_out[...], preferred_element_type=F32)
        terms = projected[:HALF] * gates[0, :1, :] + projected[HALF:] * gates[1, :1, :]
        sb[t, h] = fold(terms.reshape(8, 8, WIDTH))

    def send_terms(t, h):
        each_owner(t, h, lambda copy: copy.start())

    def own(t, h):
        @pl.when(colour == h)
        def _():
            rb[t, k] = sb[t, h, k // 2]

            came_all(rb.at[t, pl.ds(0, STEPS - 1)], s_recv.at[t])
            terms = unfold(rb[t])
            start_rows = clip_rows()
            total = jnp.zeros_like(start_rows)
            if t == 0:
                for j in range(STEPS):
                    states[j] = start_rows + total
                    total = total + (increment(j) * start_rows + terms[j])
                nb[0] = fold(layer_norm(states[...]))
            else:
                drifts = []
                for j in range(STEPS):
                    total = total + (increment(j) * states[j] + terms[j])
                    drifts.append(total)
                nb[1] = fold(jnp.stack(drifts, axis=0))

            def back(o, carry):
                back_copy(t, o).start()
                return carry

            lax.fori_loop(1, STEPS, back, 0)
            nr[t, h, k // 2] = nb[t, k]

    def rows_back(t, h):
        @pl.when(colour == h)
        def _():
            came_all(nr.at[t, h, pl.ds(0, 7)], n_recv.at[t, h])

        @pl.when(colour != h)
        def _():
            came_all(nr.at[t, h], n_recv.at[t, h])

        return unfold(nr[t, h]).reshape(HALF, WIDTH)

    def next_rows(h):
        xall[1, 0, c, half_rows(h)] = rows_back(0, h).astype(BF16)
        begin(1, h)

    def final_copy(h):
        return remote(
            nr.at[1, h], fin.at[h], pair_send.at[1 + h], pair_recv.at[1 + h], {"cfg": other}
        )

    def out_copy(rows, i):
        return pltpu.make_async_copy(
            out_rows.at[rows], out_ref.at[rows], local_sem.at[4 + i]
        )

    def own_out(h):
        rows = pl.ds(pl.multiple_of(c * CHUNK + h * HALF, HALF), HALF)
        drift = rows_back(1, h)
        final_copy(h).start()
        out_rows[rows, :] = drift.astype(BF16)
        out_copy(rows, h).start()

    def increment(j):
        return jnp.concatenate([incs[j]] * (WIDTH // 128), axis=1)

    def results_left(t):
        for h in range(2):
            left_all(ob.at[t, h, pl.ds(0, COLUMN - 1)], a2a_send.at[t, h])

    def ring_left(t):
        hops = (2, 4)[t]
        left_all(xall.at[t, pl.ds(0, hops), 0], maj_send.at[t])
        left_all(xall.at[t, pl.ds(0, min(hops, 3)), 0], min_send.at[t])
        left_all(xall.at[t, pl.ds(0, 4 if hops == 2 else RING), 0], d2d_send.at[t])

    def exchange_left(t):
        left_all(nb.at[t, pl.ds(0, STEPS - 1)], n_send.at[t])
        left_all(rb.at[t, pl.ds(0, STEPS - 1)], s_send.at[t])

    gather_first()
    loads[3].wait()
    gate_copy_back = remote(
        gates.at[other], gates.at[other], pair_send.at[0], pair_recv.at[0], {"cfg": other}
    )
    gate_copy_back.wait_recv()

    came_all(incs.at[pl.ds(0, STEPS - 1)], inc_recv.at[0])
    for h in range(2):
        merge(0, h)
        send_terms(0, h)
    for h in range(2):
        own(0, h)
    next_rows(0)
    next_rows(1)
    onward(1, 1, 0, 4)

    gate_copy.wait_send()
    ring_left(0)
    exchange_left(0)
    results_left(0)
    left_all(incs.at[pl.ds(0, STEPS - 1)], inc_send.at[0])
    left_all(far_bytes, far_send.at[0])
    left_all(one_bytes, plane_send.at[0])
    left_all(two_bytes, plane_send.at[1])
    plane_across(c).wait_send()

    gather_second()
    ring_left(1)
    for h in range(2):
        merge(1, h)
        send_terms(1, h)
    results_left(1)
    for h in range(2):
        own(1, h)
    own_out(0)
    own_out(1)
    for h in range(2):
        rows = pl.ds(pl.multiple_of(other * CHUNK + h * HALF, HALF), HALF)
        final_copy(h).wait_recv()
        out_rows[rows, :] = unfold(fin[h]).reshape(HALF, WIDTH).astype(BF16)
        out_copy(rows, 2 + h).start()
    exchange_left(1)
    for h in range(2):
        final_copy(h).wait_send()
        out_copy(half_rows(h), h).wait()
        out_copy(half_rows(h), 2 + h).wait()


def local(clip, ordinal, strength, increment, table, pair, w_in, w_merge, sharp):
    vmem = pl.BlockSpec(memory_space=pltpu.VMEM)
    smem = pl.BlockSpec(memory_space=pltpu.SMEM)
    anywhere = pl.BlockSpec(memory_space=pl.ANY)
    dma = pltpu.SemaphoreType.DMA
    out = pl.pallas_call(
        kernel,
        out_shape=jax.ShapeDtypeStruct(clip.shape, BF16),
        in_specs=[vmem, smem, smem, smem, vmem, vmem, anywhere, anywhere, smem],
        out_specs=anywhere,
        scratch_shapes=[
            pltpu.VMEM((2, RING, 2, CHUNK, WIDTH), BF16),
            pltpu.VMEM((3, WIDTH, 128), BF16),
            pltpu.VMEM((WIDTH, 384), BF16),
            pltpu.VMEM((WIDTH, WIDTH), BF16),
            pltpu.VMEM((8, 384), F32),
            pltpu.VMEM((FRAMES, 128), BF16),
            pltpu.VMEM((2, FRAMES, 128), BF16),
            pltpu.VMEM((2, 80, FRAMES), BF16),
            pltpu.VMEM((2, 80, FRAMES), F32),
            pltpu.VMEM((2, 2, COLUMN, HALF, 128), BF16),
            pltpu.VMEM((2, 2, 2, RING, HALF, 128), BF16),
            pltpu.VMEM((2, 2, 8, 16, 512), BF16),
            pltpu.VMEM((2, STEPS, 16, 512), BF16),
            pltpu.VMEM((2, STEPS, 16, 512), BF16),
            pltpu.VMEM((2, 2, 8, 16, 512), BF16),
            pltpu.VMEM((2, 8, 16, 512), BF16),
            pltpu.VMEM((STEPS, 8, WIDTH), F32),
            pltpu.VMEM((2, 8, WIDTH), F32),
            pltpu.VMEM((STEPS, 8, 128), F32),
            pltpu.VMEM((2 * CHUNK, WIDTH), BF16),
            dma((8,)),
            dma((2,)),
            dma((2,)),
            dma((2,)),
            dma((2, RING, 2, 2)),
            dma((2,)),
            dma((2,)),
            dma((2,)),
            dma((2,)),
            dma((2, 2)),
            dma((2, 2)),
            dma((2,)),
            dma((2,)),
            dma((2,)),
            dma((2, 2)),
            dma((1,)),
            dma((1,)),
            dma((3,)),
            dma((3,)),
        ],
        compiler_params=pltpu.CompilerParams(
            collective_id=0, has_side_effects=True, vmem_limit_bytes=56 * 2**20
        ),
    )(clip, ordinal, strength, increment, table, pair, w_in, w_merge, sharp)
    return (clip + out.astype(F32))[None]


def solution(mesh):
    placed = (P("seq", None), P("step"), P("step"), P("step"), P(), P("cfg", None), P(), P(), P())
    return jax.shard_map(
        local, mesh=mesh, in_specs=placed, out_specs=P("step", "seq", None), check_vma=False
    )
```
